256 devices in a mesh: dp: 32 (over z, y), mp: 8 (over x, core).
Axes of the slice: x: 4, y: 4, z: 8, core: 2. Of those that a mesh axis runs over, the one named last changes fastest.
Arguments:
- enc_context: bfloat16 [4096, 2048], P('dp', 'mp'), may hold values from -6 to 6
- enc_resid: bfloat16 [4096, 4096], P('dp', 'mp'), may hold values from -8 to 8
- enc_out_w: bfloat16 [2048, 4096], P('mp'), may hold values from -0.25 to 0.25
- final_gain: bfloat16 [4096], P('mp'), may hold values from 0.099609375 to 1.8984375
- kv_weight: bfloat16 [2, 4096, 2048], P(None, None, 'mp'), may hold values from -0.09375 to 0.09375
- img_queries: bfloat16 [4096, 2048], P('dp', 'mp'), may hold values from -48 to 48
- img_resid: bfloat16 [4096, 4096], P('dp', 'mp'), may hold values from -8 to 8
- dec_out_w: bfloat16 [2048, 4096], P('mp'), may hold values from -0.25 to 0.25
- moe_gain: bfloat16 [4096], P('mp'), may hold values from 0.099609375 to 1.8984375
- router_w: bfloat16 [4096, 32], P('mp'), may hold values from -0.1875 to 0.1875
- expert_ids: int32 [4096, 2], P('dp'), may hold values from 0 to 31, all different within a row; in each aligned block of 128 rows (0 to 127, 128 to 255, ...) at most 24 rows name the same one
- text_lengths: int32 [32], P('dp'), may hold values from 1 to 128, 2560 in all
- expert_in: bfloat16 [32, 4096, 2048], P('dp', None, 'mp'), may hold values from -0.09375 to 0.09375
- expert_out: bfloat16 [32, 2048, 4096], P('dp', 'mp'), may hold values from -0.1875 to 0.1875
Outputs:
- encoded: bfloat16 [4096, 4096], P('dp', 'mp')
- mixed: bfloat16 [4096, 4096], P('dp', 'mp')
The draws below stay inside these ranges and needn't reach their ends.
Inputs may be any that keep to these rules, and one draw needn't show every extreme that they name: `expert_ids`: the two experts of a row differ. Within each aligned block of 128 rows (one sample) no expert is named by more than 24 rows, a bound that some block of every draw reaches.
All inputs are finite; a program needn't handle non-finite values. No bound on the sum of `text_lengths` on one device may be relied on, other than what follows from the above.
Results may differ from the reference program's by a relative error of at most 0.013.
Values may be sent and summed in bfloat16 or wider, within the bound.
A program may use at most 128 MiB of HBM per device.

```python
import math
import jax
import jax.numpy as jnp
import numpy as np
from jax import lax

D = 4096
HEADS = 32
HD = 64
FF = 2048
TXT = 128
ROWS = 128
EXPERTS = 32
INNER = 2048
CAP = 24
TEXT_ALL = 4096
IMAGE_ALL = 4096
N_DP = 32


def draw_img_queries(key, part):
    key = jax.random.fold_in(key, 11)
    base = jax.random.normal(key, (N_DP * ROWS, HEADS * HD), jnp.float32)
    return jnp.clip(base, -6.0, 6.0).astype(jnp.bfloat16)


def column_scales(key, width, low, high):
    position = jnp.arange(width, dtype=jnp.float32) / width
    rising = low * jnp.exp(jnp.log(high / low) * position)
    jitter = jax.random.uniform(key, (width,), jnp.float32, 0.7, 1.3)
    return (rising * jitter)[None, :]


def residual_rows(key, count):
    base_key = jax.random.fold_in(key, 1)
    col_key = jax.random.fold_in(key, 2)
    base = jax.random.normal(base_key, (count, D), jnp.float32)
    cols = column_scales(col_key, D, 0.3, 2.1)
    return jnp.clip(base * cols, -8.0, 8.0).astype(jnp.bfloat16)


def draw_enc_resid(key, part):
    key = jax.random.fold_in(key, 23)
    return residual_rows(key, N_DP * TXT)


def draw_img_resid(key, part):
    key = jax.random.fold_in(key, 37)
    return residual_rows(key, N_DP * ROWS)


def shard_levels(own_key, dims, cuts, least, high):
    level, own = 1.0, jax.random.fold_in(own_key, 6)
    for dim, parts in cuts:
        steps = jnp.exp(jax.random.uniform(jax.random.fold_in(own, dim), (parts,), jnp.float32, least / len(cuts), high / len(cuts)))
        level = level * jnp.repeat(steps, dims[dim] // parts).reshape([-1 if axis == dim else 1 for axis in range(len(dims))])
    return level


def profile(number_of, total, most, lean):
    weights = [(1 << 20) // math.isqrt(rank ** lean) + 1 for rank in range(2, number_of + 1)]
    rest, counts = total - most - (number_of - 1), [1] * (number_of - 1)
    while rest > 0:
        free = [i for i in range(number_of - 1) if counts[i] < most]
        whole, budget = sum([weights[i] for i in free]), rest
        for i in free:
            more = min(most - counts[i], max(1, budget * weights[i] // whole), rest)
            counts[i] = counts[i] + more
            rest = rest - more
    return np.array([most] + counts)


def uneven(own_key, amount, total, most, skew):
    if amount == 2:
        one = jax.random.randint(own_key, (), max(1, total - most), min(most, total - 1) + 1)
        return jnp.stack([one, total - one])
    lengths = jnp.asarray(profile(amount, total, most, skew), jnp.int32)
    twos = (amount - 1) // 2
    source_of, sink = lengths[1:1 + 2 * twos:2], lengths[2:2 + 2 * twos:2]
    room = jnp.minimum(source_of - 1, most - sink)
    passed = jax.random.randint(jax.random.fold_in(own_key, 1), (twos,), 0, 1 << 20) % (room + 1)
    lengths = lengths.at[1:1 + 2 * twos:2].set(source_of - passed).at[2:2 + 2 * twos:2].set(sink + passed)
    return lengths[jax.random.permutation(jax.random.fold_in(own_key, 2), amount)]


def deal_out(key, own, number, rows, amount, top, bound, slope):
    sequence = jax.random.permutation(key, amount)
    heavy_load, usual = load_shares(amount, rows * top, bound, slope, True), load_shares(amount, rows * top, bound, slope, False)
    places = jnp.arange(amount)

    def named(lengths, turn):
        used = int((lengths > 0).sum())
        fixed = max(1, used // 4)
        moved = fixed + (places - fixed + turn * (used - fixed)) % max(1, amount - fixed)
        return jnp.zeros((amount,), jnp.int32).at[sequence[jnp.where(places < fixed, places, moved)]].set(jnp.asarray(lengths, jnp.int32))

    lengths = jnp.where(number % 4 == 0, named(heavy_load, number // 4), named(usual, number - number // 4 - 1))
    mixed = jax.random.permutation(jax.random.fold_in(own, 3), amount)
    donor, taker = mixed[0:amount // 2 * 2:2], mixed[1:amount // 2 * 2:2]
    margin = jnp.minimum(lengths[donor] - 1, bound - lengths[taker]) // 2
    margin = jnp.where((donor == sequence[0]) | (taker == sequence[0]) | (lengths[taker] == 0), 0, jnp.maximum(margin, 0))
    moved = jax.random.randint(jax.random.fold_in(own, 4), (amount // 2,), 0, 1 << 20) % (margin + 1)
    lengths = lengths.at[donor].add(-moved).at[taker].add(moved)
    items = jnp.searchsorted(jnp.cumsum(lengths), jnp.arange(rows * top), side="right").astype(jnp.int32)
    table = items.reshape(top, rows).T
    table = table[jax.random.permutation(jax.random.fold_in(own, 1), rows)]
    turn = jax.random.randint(jax.random.fold_in(own, 2), (rows, 1), 0, top)
    return jnp.take_along_axis(table, (jnp.arange(top)[None, :] + turn) % top, axis=1)


def load_shares(count, total, reach, lean, full):
    weights = [(1 << 20) // math.isqrt(rank ** lean) + 1 for rank in range(1, count + 1)]
    largest = reach if full else min(reach, max(-(-total // count), total * weights[0] // sum(weights)))
    least = 1 if total - largest >= count - 1 else 0
    counts, spare = [largest] + [least] * (count - 1), total - largest - least * (count - 1)
    while spare > 0:
        candidates = [i for i in range(1, count) if counts[i] < largest] or [i for i in range(1, count) if counts[i] < reach]
        mass, budget = sum([weights[i] for i in candidates]), spare
        for i in candidates:
            addition = min(reach - counts[i], max(1, budget * weights[i] // mass), spare)
            counts[i] = counts[i] + addition
            spare = spare - addition
    return np.array(counts)


def centred(own_key, dims, spread, most, split=(), held_as=jnp.bfloat16):
    drawn = spread * jax.random.normal(own_key, dims, jnp.float32)
    if split:
        drawn = drawn * shard_levels(own_key, dims, split, -0.22, 0.18)
    return jnp.clip(drawn, -most, most).astype(held_as)


def setup_inputs(seed: int = 0) -> dict:
    keys = jax.random.split(jax.random.key(seed), 15)
    enc_context = centred(keys[0], (TEXT_ALL, INNER), 1.0, 6.0, ((0, 32), (1, 8)))
    enc_resid = draw_enc_resid(jax.random.fold_in(keys[14], 71), 0)
    enc_out_w = centred(keys[2], (INNER, D), (INNER // 4) ** -0.5, 0.25, ((0, 8),))
    final_gain = jnp.clip(1.0 + 0.18 * jax.random.normal(keys[3], (D,), jnp.float32), 0.099609375, 1.8984375).astype(jnp.bfloat16)
    kv_weight = centred(keys[4], (2, D, INNER), D ** -0.5, 0.09375, ((2, 8),))
    img_queries = draw_img_queries(jax.random.fold_in(keys[14], 71), 0)
    img_resid = draw_img_resid(jax.random.fold_in(keys[14], 71), 0)
    dec_out_w = centred(keys[7], (INNER, D), (INNER // 4) ** -0.5, 0.25, ((0, 8),))
    moe_gain = jnp.clip(1.0 + 0.18 * jax.random.normal(keys[8], (D,), jnp.float32), 0.099609375, 1.8984375).astype(jnp.bfloat16)
    router_w = centred(keys[9], (D, EXPERTS), (D // 4) ** -0.5, 0.1875, ((0, 8),))
    expert_ids_keys = jax.random.split(jax.random.fold_in(keys[10], 1), IMAGE_ALL // ROWS)
    expert_ids_turns = jax.random.permutation(jax.random.fold_in(keys[10], 3), IMAGE_ALL // ROWS)
    expert_ids = jax.vmap(lambda own, number: deal_out(jax.random.fold_in(keys[10], 2), own, number, ROWS, EXPERTS, 2, CAP, 2))(expert_ids_keys, expert_ids_turns).reshape((IMAGE_ALL, 2))
    text_lengths = uneven(keys[11], N_DP, N_DP * TXT * 5 // 8, TXT, 1).astype(jnp.int32)
    expert_in = centred(keys[12], (EXPERTS, D, FF), D ** -0.5, 0.09375, ((0, 32), (2, 8)))
    expert_out = centred(keys[13], (EXPERTS, FF, D), (FF // 2) ** -0.5, 0.1875, ((0, 32), (1, 8)))
    return {"enc_context": enc_context, "enc_resid": enc_resid, "enc_out_w": enc_out_w, "final_gain": final_gain, "kv_weight": kv_weight, "img_queries": img_queries, "img_resid": img_resid, "dec_out_w": dec_out_w, "moe_gain": moe_gain, "router_w": router_w, "expert_ids": expert_ids, "text_lengths": text_lengths, "expert_in": expert_in, "expert_out": expert_out}


EPSILON = 1e-06
SCORE_SCALE = 0.125

def slot_table(expert_ids):
    pair_ids = expert_ids.reshape(N_DP, ROWS * 2)
    onehot = (pair_ids[:, :, None] == jnp.arange(EXPERTS, dtype=jnp.int32)[None, None, :]).astype(jnp.int32)
    earlier = jnp.cumsum(onehot, axis=1) - onehot
    return lax.optimization_barrier(jnp.sum(earlier * onehot, axis=2)).reshape(N_DP * ROWS * 2)

def reference(enc_context, enc_resid, enc_out_w, final_gain, kv_weight, img_queries, img_resid, dec_out_w, moe_gain, router_w, expert_ids, text_lengths, expert_in, expert_out):
    text_attn = jnp.dot(enc_context, enc_out_w, preferred_element_type=jnp.float32)
    text_state = enc_resid.astype(jnp.float32) + text_attn
    text_scale = lax.rsqrt(lax.optimization_barrier(jnp.mean(text_state * text_state, axis=1, keepdims=True)) + EPSILON)
    encoded = (text_state * final_gain.astype(jnp.float32) * text_scale).astype(jnp.bfloat16)
    key_rows = jnp.dot(encoded, kv_weight[0], preferred_element_type=jnp.float32).astype(jnp.bfloat16)
    value_rows = jnp.dot(encoded, kv_weight[1], preferred_element_type=jnp.float32).astype(jnp.bfloat16)
    query_heads = img_queries.astype(jnp.float32).reshape(N_DP, ROWS, HEADS, HD)
    key_heads = key_rows.astype(jnp.float32).reshape(N_DP, TXT, HEADS, HD)
    value_heads = value_rows.astype(jnp.float32).reshape(N_DP, TXT, HEADS, HD)
    scores = jnp.einsum('bqhd,bkhd->bhqk', query_heads, key_heads) * SCORE_SCALE
    valid = jnp.arange(TXT, dtype=jnp.int32)[None, None, None, :] < text_lengths[:, None, None, None]
    scores = jnp.where(valid, scores, -jnp.inf)
    probs = jax.nn.softmax(scores, axis=-1).astype(jnp.bfloat16)
    context = jnp.einsum('bhqk,bkhd->bqhd', probs.astype(jnp.float32), value_heads)
    context = context.reshape(IMAGE_ALL, INNER).astype(jnp.bfloat16)
    cross = jnp.dot(context, dec_out_w, preferred_element_type=jnp.float32)
    hidden = img_resid.astype(jnp.float32) + cross
    rms_scale = lax.rsqrt(lax.optimization_barrier(jnp.mean(hidden * hidden, axis=1, keepdims=True)) + EPSILON)
    gained = hidden * moe_gain.astype(jnp.float32)
    normed = (gained * rms_scale).astype(jnp.bfloat16)
    logits = rms_scale * jnp.dot(gained, router_w.astype(jnp.float32), precision=lax.Precision.HIGHEST)
    choose = (expert_ids[:, :, None] == jnp.arange(EXPERTS, dtype=jnp.int32)[None, None, :]).astype(jnp.float32)
    picked = lax.optimization_barrier(jnp.sum(choose * logits[:, None, :], axis=2))
    gates = jax.nn.softmax(picked, axis=1)
    slots = slot_table(expert_ids)
    source = jnp.repeat(jnp.arange(IMAGE_ALL, dtype=jnp.int32) // ROWS, 2)
    flat_ids = expert_ids.reshape(IMAGE_ALL * 2)
    flat_place = (source * CAP + slots).astype(jnp.int32)
    token_rows = jnp.repeat(normed, 2, axis=0)
    flat_gates = gates.reshape(IMAGE_ALL * 2)
    limit = N_DP * CAP

    def one_expert(total, inputs):
        expert_num, weight_in, weight_out = inputs
        chosen = flat_ids == expert_num
        place = jnp.where(chosen, flat_place, limit).astype(jnp.int32)
        buffer = jnp.zeros((limit, D), jnp.bfloat16).at[place].set(token_rows, mode='drop')
        inner = jax.nn.gelu(jnp.dot(buffer, weight_in, preferred_element_type=jnp.float32), approximate=True).astype(jnp.bfloat16)
        result = jnp.dot(inner, weight_out, preferred_element_type=jnp.float32)
        fetched = result[jnp.minimum(place, limit - 1)]
        weight_here = jnp.where(chosen, flat_gates, jnp.zeros_like(flat_gates))
        return (total + weight_here[:, None] * fetched, None)
    start_total = jnp.zeros((IMAGE_ALL * 2, D), jnp.float32)
    total, _ = lax.scan(one_expert, start_total, (jnp.arange(EXPERTS, dtype=jnp.int32), expert_in, expert_out))
    moe = lax.optimization_barrier(jnp.sum(total.reshape(IMAGE_ALL, 2, D), axis=1))
    mixed = (hidden + moe).astype(jnp.bfloat16)
    return (encoded, mixed)
```

```python
import functools
import jax
import jax.numpy as jnp
from jax import lax
from jax.experimental import pallas as pl
from jax.experimental.pallas import tpu as pltpu
from jax.sharding import PartitionSpec as P

HD = 64
EPSILON = 1e-06
SCORE_SCALE = 0.125
MESH = pl.DeviceIdType.MESH
NZ, NY, NX = 8, 4, 4
N_DP, N_MP = NZ * NY, NX * 2
EXPERTS = 32
WIDTH = 4096
SLICE = WIDTH // N_MP
ROWS = 128
FF_SLICE = 256
MSG_ROWS, MSG_LANES = 16, 768
HALF = SLICE // 2
CHUNKS = 8
PER = N_DP // CHUNKS
F32, BF16 = jnp.float32, jnp.bfloat16


def remote(src, dst, send, recv, device):
    return pltpu.make_async_remote_copy(
        src_ref=src, dst_ref=dst, send_sem=send, recv_sem=recv, device_id=device, device_id_type=MESH
    )


def offset_of(order):
    turn = order // NY
    odd = turn % 2
    dz = (1 - odd) * (turn // 2) + odd * (NZ - (turn + 1) // 2)
    return dz, order % NY


def moe_kernel(
    hidden, gain, stats, ids_col, ids_row, w_in_hbm, w_out_hbm,
    mixed,
    w_in, w_out, packed, full, give, kept, taken, half_l, half_r, sum_l, sum_r, done, back,
    load_sem, disp_send, disp_recv, ag_send, ag_recv, rs_send, rs_recv, ret_send, ret_recv,
):
    dp, mp = lax.axis_index("dp"), lax.axis_index("mp")
    z, y = dp // NY, dp % NY
    x, core = mp // 2, mp % 2
    x_right, x_left, x_far = (x + 1) % NX, (x + NX - 1) % NX, (x + 2) % NX
    sibling = (dp, x * 2 + 1 - core)
    right, left = (dp, x_right * 2 + core), (dp, x_left * 2 + core)
    m_right, m_left, m_far = x_right * 2 + core, x_left * 2 + core, x_far * 2 + core
    half = PER // 2

    def dest_of(order):
        dz, dy = offset_of(order)
        return ((z + dz) % NZ) * NY + (y + dy) % NY

    def origin_of(order):
        dz, dy = offset_of(order)
        return ((z + NZ - dz) % NZ) * NY + (y + NY - dy) % NY

    barrier = pltpu.get_barrier_semaphore()

    def greet(order, carry):
        pl.semaphore_signal(barrier, inc=1, device_id=(dest_of(order), mp), device_id_type=MESH)
        return carry

    lax.fori_loop(1, N_DP, greet, 0)
    for device in (sibling, right, left):
        pl.semaphore_signal(barrier, inc=1, device_id=device, device_id_type=MESH)
    load_in = pltpu.make_async_copy(w_in_hbm, w_in, load_sem.at[0])
    load_out = pltpu.make_async_copy(w_out_hbm, w_out, load_sem.at[1])
    load_in.start()
    load_out.start()

    table = jnp.transpose(jnp.concatenate([stats[...], jnp.zeros((ROWS - stats.shape[0], ROWS), F32)], axis=0))
    rms = lax.rsqrt(table[:, EXPERTS:EXPERTS + 1] / WIDTH + EPSILON)
    normed = (hidden[...] * gain[...].astype(F32) * rms).astype(BF16)

    row_at = lax.broadcasted_iota(jnp.int32, (ROWS, ROWS), 0)
    col_at = lax.broadcasted_iota(jnp.int32, (ROWS, ROWS), 1)
    expert_row = lax.broadcasted_iota(jnp.int32, (EXPERTS, ROWS), 0)
    named_row = [jnp.where(expert_row == ids_row[k:k + 1, :], 1.0, 0.0) for k in range(2)]
    earlier_row = jnp.dot(
        (named_row[0] + named_row[1]).astype(BF16),
        jnp.where(row_at < col_at, 1.0, 0.0).astype(BF16),
        preferred_element_type=F32,
    )
    message = lax.broadcasted_iota(jnp.int32, (EXPERTS * MSG_ROWS, ROWS), 0)
    upper = (message // 8) % 2
    pick_head = jnp.zeros((EXPERTS * MSG_ROWS, ROWS), F32)
    pick_tail = jnp.zeros((EXPERTS * MSG_ROWS, ROWS), F32)
    for k in range(2):
        slot = jnp.sum(named_row[k] * earlier_row, axis=0, keepdims=True).astype(jnp.int32)
        base = ids_row[k:k + 1, :] * MSG_ROWS
        head_at = jnp.where(slot < MSG_ROWS, base + slot, -1)
        tail_at = jnp.where(slot >= MSG_ROWS, base + slot - MSG_ROWS, -1)
        pick_head = pick_head + jnp.where(message == head_at, 1.0, 0.0)
        pick_tail = pick_tail + jnp.where(message - 8 * upper == tail_at, 1.0, 0.0)
    head = jnp.dot(pick_head.astype(BF16), normed, preferred_element_type=F32)
    packed[:, :, 0:SLICE] = head.astype(BF16).reshape(EXPERTS, MSG_ROWS, SLICE)
    tail = jnp.dot(pick_tail.astype(BF16), normed, preferred_element_type=F32)
    tail = jnp.where(upper[:, 0:1] == 0, tail[:, 0:HALF], tail[:, HALF:SLICE])
    packed[:, :, SLICE:MSG_LANES] = tail.astype(BF16).reshape(EXPERTS, MSG_ROWS, HALF)

    pl.semaphore_wait(barrier, N_DP - 1 + 3)

    own = pltpu.make_async_copy(packed.at[dp], full.at[mp, 0, 0], disp_recv.at[0])
    own.start()

    def dispatch(order, carry):
        dest = dest_of(order)
        chunk, place = order // PER, order % PER
        remote(packed.at[dest], full.at[mp, chunk, place], disp_send, disp_recv.at[chunk], (dest, mp)).start()
        return carry

    lax.fori_loop(1, N_DP, dispatch, 0)

    def gather_copy(kind, k):
        src = {
            0: (mp, None, sibling), 1: (mp, None, right), 2: (mp, None, left),
            3: (m_left, 0, right), 4: (m_right, half, left),
            5: (m_left, None, sibling), 6: (m_right, None, sibling), 7: (m_far, None, sibling),
        }[kind]
        place, part, device = src
        ref = full.at[place, k] if part is None else full.at[place, k, pl.ds(part, half)]
        return remote(ref, ref, ag_send.at[kind, k], ag_recv.at[kind, k], device)

    def sum_copy(kind, k):
        src, dst, device = {
            0: (give.at[k], taken.at[k], sibling),
            1: (kept.at[k, x_far, pl.ds(0, half)], half_l.at[k], right),
            2: (kept.at[k, x_far, pl.ds(half, half)], half_r.at[k], left),
            3: (kept.at[k, x_right], sum_l.at[k], right),
            4: (kept.at[k, x_left], sum_r.at[k], left),
        }[kind]
        return remote(src, dst, rs_send.at[kind, k], rs_recv.at[kind, k], device)

    def arrive(k):
        pltpu.make_async_copy(full.at[mp, k], full.at[mp, k], disp_recv.at[k]).wait()
        for kind in (1, 2, 0):
            gather_copy(kind, k).start()

    def forward(k):
        gather_copy(1, k).wait_recv()
        gather_copy(3, k).start()
        gather_copy(2, k).wait_recv()
        gather_copy(4, k).start()
        gather_copy(5, k).start()
        gather_copy(6, k).start()

    def forward_far(k):
        gather_copy(3, k).wait_recv()
        gather_copy(4, k).wait_recv()
        gather_copy(7, k).start()

    def compute(k):
        for kind in (0, 5, 6, 7):
            gather_copy(kind, k).wait_recv()

        @pl.when(k == 0)
        def _():
            load_in.wait()
            load_out.wait()

        rows = PER * MSG_ROWS
        low = jnp.zeros((2 * rows, FF_SLICE), F32)
        high = jnp.zeros((2 * rows, FF_SLICE), F32)
        for s in range(N_MP):
            block = full[s, k].reshape(rows, MSG_LANES)
            end = block[:, SLICE:]
            low = low + jnp.dot(
                jnp.concatenate([block[:, 0:HALF], end], axis=0),
                w_in[s * SLICE:s * SLICE + HALF, :],
                preferred_element_type=F32,
            )
            high = high + jnp.dot(
                jnp.concatenate([block[:, HALF:SLICE], end], axis=0),
                w_in[s * SLICE + HALF:(s + 1) * SLICE, :],
                preferred_element_type=F32,
            )
        ends = (
            low[rows:].reshape(PER, MSG_ROWS, FF_SLICE)[:, 0:8]
            + high[rows:].reshape(PER, MSG_ROWS, FF_SLICE)[:, 8:16]
        )
        before = jnp.concatenate([low[:rows] + high[:rows], ends.reshape(PER * 8, FF_SLICE)], axis=0)
        inner = jax.nn.gelu(before, approximate=True).astype(BF16)

        def result(ref, px, side):
            at = pl.multiple_of((px * 2 + side) * SLICE, SLICE)
            out = jnp.dot(inner, w_out[:, pl.ds(at, SLICE)], preferred_element_type=F32)
            ref[k, px, :, :, 0:SLICE] = out[:rows].astype(BF16).reshape(PER, MSG_ROWS, SLICE)
            ends = out[rows:].reshape(PER, 8, SLICE)
            ends = jnp.concatenate([ends[:, :, 0:HALF], ends[:, :, HALF:SLICE]], axis=1)
            ref[k, px, :, :, SLICE:MSG_LANES] = ends.astype(BF16)

        for px in range(NX):
            result(give, px, 1 - core)
        sum_copy(0, k).start()
        for px in range(NX):
            result(kept, px, core)

    def pair(k, px, part=slice(None)):
        return kept[k, px, part].astype(F32) + taken[k, px, part].astype(F32)

    def add_sibling(k):
        sum_copy(0, k).wait_recv()
        kept[k, x_far] = pair(k, x_far).astype(BF16)
        sum_copy(1, k).start()
        sum_copy(2, k).start()

    def add_far(k):
        first, second = slice(0, half), slice(half, PER)
        sum_copy(1, k).wait_recv()
        kept[k, x_right, first] = (pair(k, x_right, first) + half_l[k].astype(F32)).astype(BF16)
        kept[k, x_right, second] = pair(k, x_right, second).astype(BF16)
        sum_copy(3, k).start()
        sum_copy(2, k).wait_recv()
        kept[k, x_left, first] = pair(k, x_left, first).astype(BF16)
        kept[k, x_left, second] = (pair(k, x_left, second) + half_r[k].astype(F32)).astype(BF16)
        sum_copy(4, k).start()

    def finish(k):
        sum_copy(3, k).wait_recv()
        sum_copy(4, k).wait_recv()
        done[k] = (pair(k, x) + sum_l[k].astype(F32) + sum_r[k].astype(F32)).astype(BF16)
        for j in range(PER):
            order = k * PER + j
            origin = origin_of(order)
            if j == 0:
                @pl.when(k == 0)
                def _():
                    pltpu.make_async_copy(done.at[k, j], back.at[dp], ret_recv).start()

                @pl.when(k > 0)
                def _():
                    remote(done.at[k, j], back.at[dp], ret_send, ret_recv, (origin, mp)).start()
            else:
                remote(done.at[k, j], back.at[dp], ret_send, ret_recv, (origin, mp)).start()
        for kind in range(8):
            gather_copy(kind, k).wait_send()
        for kind in range(5):
            sum_copy(kind, k).wait_send()

    stages = (arrive, forward, forward_far, compute, add_sibling, add_far, finish)

    def step(i, carry):
        for lag, stage in enumerate(stages):
            @pl.when((i >= lag) & (i - lag < CHUNKS))
            def _():
                stage(i - lag)
        return carry

    lax.fori_loop(0, CHUNKS + len(stages) - 1, step, 0)

    expert_col = lax.broadcasted_iota(jnp.int32, (ROWS, EXPERTS), 1)
    named_col = [jnp.where(expert_col == ids_col[:, k:k + 1], 1.0, 0.0) for k in range(2)]
    earlier_col = jnp.dot(
        jnp.where(col_at < row_at, 1.0, 0.0).astype(BF16),
        (named_col[0] + named_col[1]).astype(BF16),
        preferred_element_type=F32,
    )
    logits = [rms * jnp.sum(named_col[k] * table[:, 0:EXPERTS], axis=1, keepdims=True) for k in range(2)]
    top = jnp.maximum(logits[0], logits[1])
    raised = [jnp.exp(value - top) for value in logits]
    place = lax.broadcasted_iota(jnp.int32, (ROWS, EXPERTS * MSG_ROWS), 1)
    gate_head = jnp.zeros(place.shape, F32)
    gate_low = jnp.zeros(place.shape, F32)
    gate_high = jnp.zeros(place.shape, F32)
    for k in range(2):
        gate = raised[k] / (raised[0] + raised[1])
        slot = jnp.sum(named_col[k] * earlier_col, axis=1, keepdims=True).astype(jnp.int32)
        base = ids_col[:, k:k + 1] * MSG_ROWS
        head_at = jnp.where(slot < MSG_ROWS, base + slot, -1)
        tail_at = jnp.where(slot >= MSG_ROWS, base + slot - MSG_ROWS, -100)
        gate_head = gate_head + jnp.where(place == head_at, gate, 0.0)
        gate_low = gate_low + jnp.where(place == tail_at, gate, 0.0)
        gate_high = gate_high + jnp.where(place == tail_at + 8, gate, 0.0)

    pltpu.make_async_copy(back, back, ret_recv).wait()

    def weigh(weights, values):
        main = weights.astype(BF16)
        rest = (weights - main.astype(F32)).astype(BF16)
        return jnp.dot(main, values, preferred_element_type=F32) + jnp.dot(
            rest, values, preferred_element_type=F32
        )

    results = back[...].reshape(EXPERTS * MSG_ROWS, MSG_LANES)
    ends = results[:, SLICE:]
    moe = weigh(gate_head, results[:, 0:SLICE])
    mixed[:, 0:HALF] = (hidden[:, 0:HALF] + moe[:, 0:HALF] + weigh(gate_low, ends)).astype(BF16)
    mixed[:, HALF:] = (hidden[:, HALF:] + moe[:, HALF:] + weigh(gate_high, ends)).astype(BF16)

    most = packed.at[pl.ds(0, N_DP - 1)]
    remote(most, most, disp_send, disp_recv.at[0], sibling).wait_send()
    remote(most, most, ret_send, ret_recv, sibling).wait_send()


def moe_call(hidden, gain, stats, ids, w_in, w_out):
    block = (PER, MSG_ROWS, MSG_LANES)
    vmem = pl.BlockSpec(memory_space=pltpu.VMEM)
    hbm = pl.BlockSpec(memory_space=pl.ANY)
    dma = pltpu.SemaphoreType.DMA
    return pl.pallas_call(
        moe_kernel,
        out_shape=jax.ShapeDtypeStruct((ROWS, SLICE), BF16),
        in_specs=[vmem] * 5 + [hbm] * 2,
        out_specs=vmem,
        scratch_shapes=[
            pltpu.VMEM((WIDTH, FF_SLICE), BF16),
            pltpu.VMEM((FF_SLICE, WIDTH), BF16),
            pltpu.VMEM((EXPERTS, MSG_ROWS, MSG_LANES), BF16),
            pltpu.VMEM((N_MP, CHUNKS) + block, BF16),
            pltpu.VMEM((CHUNKS, NX) + block, BF16),
            pltpu.VMEM((CHUNKS, NX) + block, BF16),
            pltpu.VMEM((CHUNKS, NX) + block, BF16),
            pltpu.VMEM((CHUNKS, PER // 2, MSG_ROWS, MSG_LANES), BF16),
            pltpu.VMEM((CHUNKS, PER // 2, MSG_ROWS, MSG_LANES), BF16),
            pltpu.VMEM((CHUNKS,) + block, BF16),
            pltpu.VMEM((CHUNKS,) + block, BF16),
            pltpu.VMEM((CHUNKS,) + block, BF16),
            pltpu.VMEM((EXPERTS, MSG_ROWS, MSG_LANES), BF16),
            dma((2,)),
            dma,
            dma((CHUNKS,)),
            dma((8, CHUNKS)),
            dma((8, CHUNKS)),
            dma((5, CHUNKS)),
            dma((5, CHUNKS)),
            dma,
            dma,
        ],
        compiler_params=pltpu.CompilerParams(
            collective_id=2, has_side_effects=True, vmem_limit_bytes=56 * 2**20
        ),
        name="experts",
    )(hidden, gain.reshape(1, SLICE), stats, ids, ids.T, w_in, w_out)


def local(
    enc_context, enc_resid, enc_out_w, final_gain, kv_weight, img_queries, img_resid, dec_out_w,
    moe_gain, router_w, expert_ids, text_lengths, expert_in, expert_out,
):
    full_width = enc_out_w.shape[1]
    text_part = jnp.dot(enc_context, enc_out_w, preferred_element_type=jnp.float32)
    text_state = enc_resid.astype(jnp.float32) + lax.psum_scatter(
        text_part, "mp", scatter_dimension=1, tiled=True
    )
    text_square = lax.psum(jnp.sum(text_state * text_state, axis=1), "mp")
    text_scale = lax.rsqrt(text_square / full_width + EPSILON)
    encoded = (text_state * final_gain.astype(jnp.float32) * text_scale[:, None]).astype(
        jnp.bfloat16
    )
    heads_width = kv_weight.shape[2]
    text_count = encoded.shape[0]
    kv_sums = jnp.einsum(
        "tf,cfh->cth",
        lax.all_gather(encoded, "mp", axis=1, tiled=True),
        kv_weight,
        preferred_element_type=jnp.float32,
    )
    key_rows = kv_sums[0].astype(jnp.bfloat16)
    value_rows = kv_sums[1].astype(jnp.bfloat16)
    row_count = img_queries.shape[0]
    head_count = heads_width // HD
    query_heads = img_queries.reshape(row_count, head_count, HD)
    key_heads = key_rows.reshape(text_count, head_count, HD)
    value_heads = value_rows.reshape(text_count, head_count, HD)
    scores = (
        jnp.einsum("qhd,khd->hqk", query_heads, key_heads, preferred_element_type=jnp.float32)
        * SCORE_SCALE
    )
    valid = jnp.arange(text_count, dtype=jnp.int32)[None, None, :] < text_lengths[0]
    scores = jnp.where(valid, scores, -jnp.inf)
    probs = jax.nn.softmax(scores, axis=-1).astype(jnp.bfloat16)
    context = jnp.einsum("hqk,khd->qhd", probs, value_heads, preferred_element_type=jnp.float32)
    context = context.reshape(row_count, heads_width).astype(jnp.bfloat16)
    cross_part = jnp.dot(context, dec_out_w, preferred_element_type=jnp.float32)
    hidden = img_resid.astype(jnp.float32) + lax.psum_scatter(
        cross_part, "mp", scatter_dimension=1, tiled=True
    )
    gained = hidden * moe_gain.astype(jnp.float32)
    square_part = jnp.sum(hidden * hidden, axis=1)
    logit_part = jnp.dot(gained, router_w.astype(jnp.float32), precision=lax.Precision.HIGHEST)
    part = jnp.concatenate(
        [logit_part.T, square_part[None, :], jnp.zeros((7, row_count), jnp.float32)], axis=0
    )
    stats = lax.psum(part, "mp")
    mixed = moe_call(hidden, moe_gain, stats, expert_ids, expert_in[0], expert_out[0])
    return (encoded, mixed)


def solution(mesh):
    placed = (
        P("dp", "mp"),
        P("dp", "mp"),
        P("mp", None),
        P("mp"),
        P(None, None, "mp"),
        P("dp", "mp"),
        P("dp", "mp"),
        P("mp", None),
        P("mp"),
        P("mp", None),
        P("dp", None),
        P("dp"),
        P("dp", None, "mp"),
        P("dp", "mp", None),
    )
    return jax.shard_map(
        local, mesh=mesh, in_specs=placed, out_specs=(P("dp", "mp"), P("dp", "mp")), check_vma=False
    )
```

```python
import functools
import jax
import jax.numpy as jnp
from jax import lax
from jax.experimental import pallas as pl
from jax.experimental.pallas import tpu as pltpu
from jax.sharding import PartitionSpec as P

HD = 64
EPSILON = 1e-06
SCORE_SCALE = 0.125
MESH = pl.DeviceIdType.MESH
NZ, NY, NX = 8, 4, 4
N_DP, N_MP = NZ * NY, NX * 2
EXPERTS = 32
WIDTH = 4096
SLICE = WIDTH // N_MP
ROWS = 128
FF_SLICE = 256
MSG_ROWS, MSG_LANES = 16, 768
HALF = SLICE // 2
CHUNKS = 8
PER = N_DP // CHUNKS
F32, BF16 = jnp.float32, jnp.bfloat16
VMEM_LIMIT = 56 * 2**20


def remote(src, dst, send, recv, device):
    return pltpu.make_async_remote_copy(
        src_ref=src, dst_ref=dst, send_sem=send, recv_sem=recv, device_id=device, device_id_type=MESH
    )


def offset_of(order):
    turn, place = order // PER, order % PER
    kind, odd = turn % 2, place % 2
    reach = 1 + kind + 2 * (place // 2)
    dz = ((1 - odd) * reach + odd * (NZ - reach)) * (1 - kind * (place // 3))
    return dz, turn // 2


PARTS = 2
PART = ROWS // PARTS
STATS = 40
AHEAD = 3
SELF = 7
LAGS = (0, 1, 2, 3, 4, 5, 6)


def kernel(*refs):
    sources, rest = refs[:14], refs[14:]
    (
        encoded, mixed,
        enc_context, enc_w, enc_resid, final_gain, kv_w, router, ids_row, img_queries, img_resid, moe_gain,
        lengths, dec_w, w_in, w_out,
        state, gathered, squares, tables, hidden, router_wide, picks, gated,
        enc_give, enc_kept, enc_taken, enc_half_l, enc_half_r, enc_sum_l, enc_sum_r,
        dec_give, dec_kept, dec_taken, dec_half_l, dec_half_r, dec_sum_l, dec_sum_r,
        packed, full, give, kept, taken, half_l, half_r, sum_l, sum_r, done, back,
        load_sem, enc_send, enc_recv, dec_send, dec_recv, ag_send, ag_recv,
        square_send, square_recv, table_send, table_recv,
        disp_send, disp_recv, slot_send, slot_recv, rs_send, rs_recv, ret_send, ret_recv,
    ) = rest
    targets = rest[2:16]
    dp, mp = lax.axis_index("dp"), lax.axis_index("mp")
    z, y = dp // NY, dp % NY
    x, core = mp // 2, mp % 2
    x_right, x_left, x_far = (x + 1) % NX, (x + NX - 1) % NX, (x + 2) % NX
    m_right, m_left, m_far = x_right * 2 + core, x_left * 2 + core, x_far * 2 + core
    sibling, right, left = (dp, x * 2 + 1 - core), (dp, m_right), (dp, m_left)

    def dest_of(order):
        dz, dy = offset_of(order)
        return ((z + dz) % NZ) * NY + (y + dy) % NY

    def origin_of(order):
        dz, dy = offset_of(order)
        return ((z + NZ - dz) % NZ) * NY + (y + NY - dy) % NY

    loads = [
        pltpu.make_async_copy(src, dst, load_sem.at[i])
        for i, (src, dst) in enumerate(zip(sources, targets))
    ]
    for load in loads[:3]:
        load.start()
    barrier = pltpu.get_barrier_semaphore()
    for o in range(1, N_MP):
        pl.semaphore_signal(barrier, inc=1, device_id=(dp, (mp + o) % N_MP), device_id_type=MESH)

    def greet(order, carry):
        pl.semaphore_signal(barrier, inc=1, device_id=(dest_of(order), mp), device_id_type=MESH)
        return carry

    lax.fori_loop(0, SELF, greet, 0)
    lax.fori_loop(SELF + 1, N_DP, greet, 0)
    for load in loads[3:]:
        load.start()

    def reduce_scatter(values, weights, resid, out, give, kept, taken, half_l, half_r, sum_l, sum_r, send, recv):
        half = PART // 2

        def copy(kind, r):
            src, dst, device = {
                0: (give.at[r], taken.at[r], sibling),
                1: (kept.at[r, x_far, pl.ds(0, half)], half_l.at[r], right),
                2: (kept.at[r, x_far, pl.ds(half, half)], half_r.at[r], left),
                3: (kept.at[r, x_right], sum_l.at[r], right),
                4: (kept.at[r, x_left], sum_r.at[r], left),
            }[kind]
            return remote(src, dst, send.at[kind, r], recv.at[kind, r], device)

        def product(ref, r, px, side):
            at = pl.multiple_of((px * 2 + side) * SLICE, SLICE)
            ref[r, px] = jnp.dot(
                values[r * PART:(r + 1) * PART], weights[:, pl.ds(at, SLICE)], preferred_element_type=F32
            ).astype(BF16)

        def pair(r, px, rows=slice(None)):
            return kept[r, px, rows].astype(F32) + taken[r, px, rows].astype(F32)

        for r in range(PARTS):
            for px in range(NX):
                product(give, r, px, 1 - core)
            if r == 0 and out is state:
                pl.semaphore_wait(barrier, N_MP - 1 + N_DP - 1)
            copy(0, r).start()
        for r in range(PARTS):
            for px in range(NX):
                product(kept, r, px, core)
        for r in range(PARTS):
            copy(0, r).wait_recv()
            kept[r, x_far] = pair(r, x_far).astype(BF16)
            copy(1, r).start()
            copy(2, r).start()
        first, second = slice(0, half), slice(half, PART)
        for r in range(PARTS):
            copy(1, r).wait_recv()
            kept[r, x_right, first] = (pair(r, x_right, first) + half_l[r].astype(F32)).astype(BF16)
            kept[r, x_right, second] = pair(r, x_right, second).astype(BF16)
            copy(3, r).start()
            copy(2, r).wait_recv()
            kept[r, x_left, first] = pair(r, x_left, first).astype(BF16)
            kept[r, x_left, second] = (pair(r, x_left, second) + half_r[r].astype(F32)).astype(BF16)
            copy(4, r).start()
        for r in range(PARTS):
            rows = slice(r * PART, (r + 1) * PART)
            base = resid[rows].astype(F32) + pair(r, x)
            copy(3, r).wait_recv()
            copy(4, r).wait_recv()
            out[rows] = base + sum_l[r].astype(F32) + sum_r[r].astype(F32)
            yield r

        def drain():
            for r in range(PARTS):
                for kind in range(5):
                    copy(kind, r).wait_send()

        drains.append(drain)

    drains = []

    def exchange(ref, send, recv):
        def copy(o):
            return remote(ref.at[mp], ref.at[mp], send.at[o], recv.at[mp], (dp, (mp + o) % N_MP))

        for o in range(1, N_MP):
            copy(o).start()

        def finish():
            for o in range(1, N_MP):
                other = ref.at[(mp + o) % N_MP]
                remote(other, other, send.at[o], recv.at[(mp + o) % N_MP], sibling).wait_recv()
            drains.append(lambda: [copy(o).wait_send() for o in range(1, N_MP)])

        return finish

    def gather_copy(kind):
        ref, device = {
            0: (gathered.at[mp, 0], sibling), 1: (gathered.at[mp, 1], sibling),
            2: (gathered.at[mp, 0], right), 3: (gathered.at[mp, 1], right),
            4: (gathered.at[mp, 0], left), 5: (gathered.at[mp, 1], left),
            6: (gathered.at[m_left, 0], right), 7: (gathered.at[m_right, 1], left),
            8: (gathered.at[m_left], sibling), 9: (gathered.at[m_right], sibling),
            10: (gathered.at[m_far], sibling),
        }[kind]
        return remote(ref, ref, ag_send.at[kind], ag_recv.at[kind], device)

    for load in loads[:4]:
        load.wait()
    text_gain = final_gain[...].astype(F32).reshape(1, SLICE)
    for r in reduce_scatter(
        enc_context[...], enc_w, enc_resid, state, enc_give, enc_kept, enc_taken, enc_half_l, enc_half_r,
        enc_sum_l, enc_sum_r, enc_send, enc_recv,
    ):
        gathered[mp, r] = (state[r * PART:(r + 1) * PART] * text_gain).astype(BF16)
        for kind in ((2, 4, 0), (5, 3, 1))[r]:
            gather_copy(kind).start()
    text_state = state[...]
    square = jnp.sum(text_state * text_state, axis=1, keepdims=True)
    squares[mp] = jnp.transpose(jnp.broadcast_to(square, (ROWS, ROWS)))[0:8]
    squares_done = exchange(squares, square_send, square_recv)

    for load in loads[4:]:
        load.wait()
    row_at = lax.broadcasted_iota(jnp.int32, (ROWS, ROWS), 0)
    col_at = lax.broadcasted_iota(jnp.int32, (ROWS, ROWS), 1)
    expert_row = lax.broadcasted_iota(jnp.int32, (EXPERTS, ROWS), 0)
    named_row = [jnp.where(expert_row == ids_row[k:k + 1, :], 1.0, 0.0) for k in range(2)]
    earlier_row = jnp.dot(
        (named_row[0] + named_row[1]).astype(BF16),
        jnp.where(row_at < col_at, 1.0, 0.0).astype(BF16),
        preferred_element_type=F32,
    )
    message = lax.broadcasted_iota(jnp.int32, (EXPERTS * MSG_ROWS, ROWS), 0)
    upper = (message // 8) % 2
    pick_head = jnp.zeros((EXPERTS * MSG_ROWS, ROWS), F32)
    pick_tail = jnp.zeros((EXPERTS * MSG_ROWS, ROWS), F32)
    slots = []
    for k in range(2):
        slot = jnp.sum(named_row[k] * earlier_row, axis=0, keepdims=True).astype(jnp.int32)
        slots.append(slot.astype(F32))
        base = ids_row[k:k + 1, :] * MSG_ROWS
        head_at = jnp.where(slot < MSG_ROWS, base + slot, -1)
        tail_at = jnp.where(slot >= MSG_ROWS, base + slot - MSG_ROWS, -1)
        pick_head = pick_head + jnp.where(message == head_at, 1.0, 0.0)
        pick_tail = pick_tail + jnp.where(message - 8 * upper == tail_at, 1.0, 0.0)
    picks[0] = pick_head.astype(BF16)
    picks[1] = pick_tail.astype(BF16)
    columns = jnp.transpose(
        jnp.concatenate([ids_row[...].astype(F32)] + slots + [jnp.zeros((ROWS - 4, ROWS), F32)], axis=0)
    )
    id_cols = [columns[:, k:k + 1].astype(jnp.int32) for k in range(2)]
    slot_cols = [columns[:, 2 + k:3 + k].astype(jnp.int32) for k in range(2)]
    router_wide[...] = jnp.zeros(router_wide.shape, F32)
    router_wide[0:EXPERTS] = router[...].astype(F32)

    sums = [jnp.zeros((ROWS, FF_SLICE), F32) for _ in range(2)]

    def project(m):
        at = pl.multiple_of(m * SLICE, SLICE)
        block = gathered[m].reshape(ROWS, SLICE)
        for which in range(2):
            sums[which] = sums[which] + jnp.dot(
                block, kv_w[which, pl.ds(at, SLICE), :], preferred_element_type=F32
            )

    project(mp)
    gather_copy(2).wait_recv()
    gather_copy(6).start()
    gather_copy(5).wait_recv()
    gather_copy(7).start()
    gather_copy(3).wait_recv()
    gather_copy(8).start()
    gather_copy(4).wait_recv()
    gather_copy(9).start()
    project(m_left)
    project(m_right)
    gather_copy(0).wait_recv()
    gather_copy(1).wait_recv()
    project(x * 2 + 1 - core)
    gather_copy(6).wait_recv()
    gather_copy(7).wait_recv()
    gather_copy(10).start()
    project(m_far)
    for kind, px in ((8, x_left), (9, x_right), (10, x_far)):
        gather_copy(kind).wait_recv()
        project(px * 2 + 1 - core)
    squares_done()
    total = squares[0]
    for m in range(1, N_MP):
        total = total + squares[m]
    total = jnp.transpose(jnp.concatenate([total, jnp.zeros((ROWS - 8, ROWS), F32)], axis=0))[:, 0:1]
    text_scale = lax.rsqrt(total / WIDTH + EPSILON)
    encoded[...] = (state[...] * text_gain * text_scale).astype(BF16)
    keys = (sums[0] * text_scale).astype(BF16)
    values = (sums[1] * text_scale).astype(BF16)

    heads = FF_SLICE // HD
    head_of = lax.broadcasted_iota(jnp.int32, (ROWS, FF_SLICE), 1) // HD
    queries = img_queries[...]
    alone = jnp.concatenate([jnp.where(head_of == h, queries, jnp.zeros_like(queries)) for h in range(heads)], axis=0)
    scores = SCORE_SCALE * lax.dot_general(
        alone, keys, (((1,), (1,)), ((), ())), preferred_element_type=F32
    )
    valid = lax.broadcasted_iota(jnp.int32, scores.shape, 1) < lengths[0]
    scores = jnp.where(valid, scores, -jnp.inf)
    raised = jnp.exp(scores - jnp.max(scores, axis=1, keepdims=True))
    probs = (raised / jnp.sum(raised, axis=1, keepdims=True)).astype(BF16)
    mixed_heads = jnp.dot(probs, values, preferred_element_type=F32)
    context = jnp.zeros((ROWS, FF_SLICE), F32)
    for h in range(heads):
        context = context + jnp.where(head_of == h, mixed_heads[h * ROWS:(h + 1) * ROWS], 0.0)
    context = context.astype(BF16)

    for _ in reduce_scatter(
        context, dec_w, img_resid, hidden, dec_give, dec_kept, dec_taken, dec_half_l, dec_half_r,
        dec_sum_l, dec_sum_r, dec_send, dec_recv,
    ):
        pass
    here = hidden[...]
    gained = here * moe_gain[...].astype(F32).reshape(1, SLICE)
    square = jnp.sum(here * here, axis=1, keepdims=True)
    logits = lax.dot_general(
        gained, router_wide[...], (((1,), (1,)), ((), ())),
        precision=lax.Precision.HIGHEST, preferred_element_type=F32,
    )
    lane = lax.broadcasted_iota(jnp.int32, (ROWS, ROWS), 1)
    tables[mp] = jnp.transpose(jnp.where(lane == EXPERTS, square, logits))[0:STATS]
    exchange(tables, table_send, table_recv)()
    total = tables[0]
    for m in range(1, N_MP):
        total = total + tables[m]
    table = jnp.transpose(jnp.concatenate([total, jnp.zeros((ROWS - STATS, ROWS), F32)], axis=0))
    rms = lax.rsqrt(table[:, EXPERTS:EXPERTS + 1] / WIDTH + EPSILON)
    normed = (gained * rms).astype(BF16)
    head = jnp.dot(picks[0], normed, preferred_element_type=F32)
    packed[:, :, 0:SLICE] = head.astype(BF16).reshape(EXPERTS, MSG_ROWS, SLICE)
    tail = jnp.dot(picks[1], normed, preferred_element_type=F32)
    upper = (lax.broadcasted_iota(jnp.int32, (EXPERTS * MSG_ROWS, ROWS), 0) // 8) % 2
    tail = jnp.where(upper[:, 0:1] == 0, tail[:, 0:HALF], tail[:, HALF:SLICE])
    packed[:, :, SLICE:MSG_LANES] = tail.astype(BF16).reshape(EXPERTS, MSG_ROWS, HALF)


    own = pltpu.make_async_copy(packed.at[dp], full.at[mp, SELF // PER, SELF % PER], disp_recv.at[SELF // PER])
    own.start()

    def dispatch(order, carry):
        dest = dest_of(order)
        chunk, place = order // PER, order % PER
        remote(packed.at[dest], full.at[mp, chunk, place], disp_send, disp_recv.at[chunk], (dest, mp)).start()
        return carry

    lax.fori_loop(0, SELF, dispatch, 0)
    lax.fori_loop(SELF + 1, AHEAD * PER, dispatch, 0)

    expert_col = lax.broadcasted_iota(jnp.int32, (ROWS, EXPERTS), 1)
    named_col = [jnp.where(expert_col == id_cols[k], 1.0, 0.0) for k in range(2)]
    logits = [rms * jnp.sum(named_col[k] * table[:, 0:EXPERTS], axis=1, keepdims=True) for k in range(2)]
    top = jnp.maximum(logits[0], logits[1])
    raised = [jnp.exp(value - top) for value in logits]
    place = lax.broadcasted_iota(jnp.int32, (ROWS, EXPERTS * MSG_ROWS), 1)
    gate_head = jnp.zeros(place.shape, F32)
    gate_low = jnp.zeros(place.shape, F32)
    gate_high = jnp.zeros(place.shape, F32)
    for k in range(2):
        gate = raised[k] / (raised[0] + raised[1])
        slot = slot_cols[k]
        base = id_cols[k] * MSG_ROWS
        head_at = jnp.where(slot < MSG_ROWS, base + slot, -1)
        tail_at = jnp.where(slot >= MSG_ROWS, base + slot - MSG_ROWS, -100)
        gate_head = gate_head + jnp.where(place == head_at, gate, 0.0)
        gate_low = gate_low + jnp.where(place == tail_at, gate, 0.0)
        gate_high = gate_high + jnp.where(place == tail_at + 8, gate, 0.0)

    for i, weights in enumerate((gate_head, gate_low, gate_high)):
        main = weights.astype(BF16)
        gated[2 * i] = main
        gated[2 * i + 1] = (weights - main.astype(F32)).astype(BF16)

    half = PER // 2

    def slot_copy(kind, k):
        src = {
            0: (mp, None, sibling), 1: (mp, None, right), 2: (mp, None, left),
            3: (m_left, 0, right), 4: (m_right, half, left),
            5: (m_left, None, sibling), 6: (m_right, None, sibling), 7: (m_far, None, sibling),
        }[kind]
        place, part, device = src
        ref = full.at[place, k] if part is None else full.at[place, k, pl.ds(part, half)]
        return remote(ref, ref, slot_send.at[kind, k], slot_recv.at[kind, k], device)

    def sum_copy(kind, k):
        src, dst, device = {
            0: (give.at[k], taken.at[k], sibling),
            1: (kept.at[k, x_far, pl.ds(0, half)], half_l.at[k], right),
            2: (kept.at[k, x_far, pl.ds(half, half)], half_r.at[k], left),
            3: (kept.at[k, x_right], sum_l.at[k], right),
            4: (kept.at[k, x_left], sum_r.at[k], left),
        }[kind]
        return remote(src, dst, rs_send.at[kind, k], rs_recv.at[kind, k], device)

    def arrive(k):
        @pl.when(k + AHEAD < CHUNKS)
        def _():
            first = (k + AHEAD) * PER
            lax.fori_loop(first, first + PER, dispatch, 0)

        pltpu.make_async_copy(full.at[mp, k], full.at[mp, k], disp_recv.at[k]).wait()
        for kind in (1, 2, 0):
            slot_copy(kind, k).start()

    def forward(k):
        slot_copy(1, k).wait_recv()
        slot_copy(3, k).start()
        slot_copy(2, k).wait_recv()
        slot_copy(4, k).start()
        slot_copy(5, k).start()
        slot_copy(6, k).start()

    def forward_far(k):
        slot_copy(3, k).wait_recv()
        slot_copy(4, k).wait_recv()
        slot_copy(7, k).start()

    def compute(k):
        for kind in (0, 5, 6, 7):
            slot_copy(kind, k).wait_recv()

        rows = PER * MSG_ROWS
        low = jnp.zeros((2 * rows, FF_SLICE), F32)
        high = jnp.zeros((2 * rows, FF_SLICE), F32)
        for s in range(N_MP):
            block = full[s, k].reshape(rows, MSG_LANES)
            end = block[:, SLICE:]
            low = low + jnp.dot(
                jnp.concatenate([block[:, 0:HALF], end], axis=0),
                w_in[s * SLICE:s * SLICE + HALF, :],
                preferred_element_type=F32,
            )
            high = high + jnp.dot(
                jnp.concatenate([block[:, HALF:SLICE], end], axis=0),
                w_in[s * SLICE + HALF:(s + 1) * SLICE, :],
                preferred_element_type=F32,
            )
        ends = (
            low[rows:].reshape(PER, MSG_ROWS, FF_SLICE)[:, 0:8]
            + high[rows:].reshape(PER, MSG_ROWS, FF_SLICE)[:, 8:16]
        )
        before = jnp.concatenate([low[:rows] + high[:rows], ends.reshape(PER * 8, FF_SLICE)], axis=0)
        inner = jax.nn.gelu(before, approximate=True).astype(BF16)

        def result(ref, px, side):
            at = pl.multiple_of((px * 2 + side) * SLICE, SLICE)
            out = jnp.dot(inner, w_out[:, pl.ds(at, SLICE)], preferred_element_type=F32)
            ref[k, px, :, :, 0:SLICE] = out[:rows].astype(BF16).reshape(PER, MSG_ROWS, SLICE)
            ends = out[rows:].reshape(PER, 8, SLICE)
            ends = jnp.concatenate([ends[:, :, 0:HALF], ends[:, :, HALF:SLICE]], axis=1)
            ref[k, px, :, :, SLICE:MSG_LANES] = ends.astype(BF16)

        for px in range(NX):
            result(give, px, 1 - core)
        sum_copy(0, k).start()
        for px in range(NX):
            result(kept, px, core)

    def pair(k, px, part=slice(None)):
        return kept[k, px, part].astype(F32) + taken[k, px, part].astype(F32)

    def add_sibling(k):
        sum_copy(0, k).wait_recv()
        kept[k, x_far] = pair(k, x_far).astype(BF16)
        sum_copy(1, k).start()
        sum_copy(2, k).start()

    def add_far(k):
        first, second = slice(0, half), slice(half, PER)
        sum_copy(1, k).wait_recv()
        kept[k, x_right, first] = (pair(k, x_right, first) + half_l[k].astype(F32)).astype(BF16)
        kept[k, x_right, second] = pair(k, x_right, second).astype(BF16)
        sum_copy(3, k).start()
        sum_copy(2, k).wait_recv()
        kept[k, x_left, first] = pair(k, x_left, first).astype(BF16)
        kept[k, x_left, second] = (pair(k, x_left, second) + half_r[k].astype(F32)).astype(BF16)
        sum_copy(4, k).start()

    def finish(k):
        sum_copy(3, k).wait_recv()
        sum_copy(4, k).wait_recv()
        done[k] = (pair(k, x) + sum_l[k].astype(F32) + sum_r[k].astype(F32)).astype(BF16)
        for j in range(PER):
            order = k * PER + j
            origin = origin_of(order)
            if j == SELF % PER:
                @pl.when(order == SELF)
                def _():
                    pltpu.make_async_copy(done.at[k, j], back.at[dp], ret_recv).start()

                @pl.when(order != SELF)
                def _():
                    remote(done.at[k, j], back.at[dp], ret_send, ret_recv, (origin, mp)).start()
            else:
                remote(done.at[k, j], back.at[dp], ret_send, ret_recv, (origin, mp)).start()
        for kind in range(8):
            slot_copy(kind, k).wait_send()
        for kind in range(5):
            sum_copy(kind, k).wait_send()

    stages = (arrive, forward, forward_far, compute, add_sibling, add_far, finish)

    def step(i, carry):
        for lag, stage in zip(LAGS, stages):
            @pl.when((i >= lag) & (i - lag < CHUNKS))
            def _():
                stage(i - lag)
        return carry

    lax.fori_loop(0, CHUNKS + LAGS[-1], step, 0)

    pltpu.make_async_copy(back, back, ret_recv).wait()

    def weigh(i, values):
        return jnp.dot(gated[2 * i], values, preferred_element_type=F32) + jnp.dot(
            gated[2 * i + 1], values, preferred_element_type=F32
        )

    results = back[...].reshape(EXPERTS * MSG_ROWS, MSG_LANES)
    ends = results[:, SLICE:]
    moe = weigh(0, results[:, 0:SLICE])
    mixed[:, 0:HALF] = (hidden[:, 0:HALF] + moe[:, 0:HALF] + weigh(1, ends)).astype(BF16)
    mixed[:, HALF:] = (hidden[:, HALF:] + moe[:, HALF:] + weigh(2, ends)).astype(BF16)

    most = packed.at[pl.ds(0, N_DP - 1)]
    remote(most, most, disp_send, disp_recv.at[0], sibling).wait_send()
    remote(most, most, ret_send, ret_recv, sibling).wait_send()


    for drain in drains:
        drain()
    for kind in range(11):
        gather_copy(kind).wait_send()


def call(*operands):
    vmem = pl.BlockSpec(memory_space=pltpu.VMEM)
    hbm = pl.BlockSpec(memory_space=pltpu.HBM)
    dma = pltpu.SemaphoreType.DMA
    block = (PER, MSG_ROWS, MSG_LANES)
    sums = [
        pltpu.VMEM((PARTS, NX, PART, SLICE), BF16),
        pltpu.VMEM((PARTS, NX, PART, SLICE), BF16),
        pltpu.VMEM((PARTS, NX, PART, SLICE), BF16),
        pltpu.VMEM((PARTS, PART // 2, SLICE), BF16),
        pltpu.VMEM((PARTS, PART // 2, SLICE), BF16),
        pltpu.VMEM((PARTS, PART, SLICE), BF16),
        pltpu.VMEM((PARTS, PART, SLICE), BF16),
    ]
    landing = [
        pltpu.SMEM(o.shape, o.dtype) if o.shape == (1,) else pltpu.VMEM(o.shape, o.dtype) for o in operands
    ]
    return pl.pallas_call(
        kernel,
        out_shape=(jax.ShapeDtypeStruct((ROWS, SLICE), BF16), jax.ShapeDtypeStruct((ROWS, SLICE), BF16)),
        in_specs=[hbm] * len(operands),
        out_specs=(vmem, vmem),
        scratch_shapes=landing + [
            pltpu.VMEM((ROWS, SLICE), F32),
            pltpu.VMEM((N_MP, PARTS, PART, SLICE), BF16),
            pltpu.VMEM((N_MP, 8, ROWS), F32),
            pltpu.VMEM((N_MP, STATS, ROWS), F32),
            pltpu.VMEM((ROWS, SLICE), F32),
            pltpu.VMEM((ROWS, SLICE), F32),
            pltpu.VMEM((2, EXPERTS * MSG_ROWS, ROWS), BF16),
            pltpu.VMEM((6, ROWS, EXPERTS * MSG_ROWS), BF16),
        ] + sums + sums + [
            pltpu.VMEM((EXPERTS, MSG_ROWS, MSG_LANES), BF16),
            pltpu.VMEM((N_MP, CHUNKS) + block, BF16),
            pltpu.VMEM((CHUNKS, NX) + block, BF16),
            pltpu.VMEM((CHUNKS, NX) + block, BF16),
            pltpu.VMEM((CHUNKS, NX) + block, BF16),
            pltpu.VMEM((CHUNKS, PER // 2, MSG_ROWS, MSG_LANES), BF16),
            pltpu.VMEM((CHUNKS, PER // 2, MSG_ROWS, MSG_LANES), BF16),
            pltpu.VMEM((CHUNKS,) + block, BF16),
            pltpu.VMEM((CHUNKS,) + block, BF16),
            pltpu.VMEM((CHUNKS,) + block, BF16),
            pltpu.VMEM((EXPERTS, MSG_ROWS, MSG_LANES), BF16),
            dma((len(operands),)),
            dma((5, PARTS)),
            dma((5, PARTS)),
            dma((5, PARTS)),
            dma((5, PARTS)),
            dma((11,)),
            dma((11,)),
            dma((N_MP,)),
            dma((N_MP,)),
            dma((N_MP,)),
            dma((N_MP,)),
            dma,
            dma((CHUNKS,)),
            dma((8, CHUNKS)),
            dma((8, CHUNKS)),
            dma((5, CHUNKS)),
            dma((5, CHUNKS)),
            dma,
            dma,
        ],
        compiler_params=pltpu.CompilerParams(
            collective_id=1, has_side_effects=True, vmem_limit_bytes=VMEM_LIMIT
        ),
        name="whole",
    )(*operands)


def local(
    enc_context, enc_resid, enc_out_w, final_gain, kv_weight, img_queries, img_resid, dec_out_w,
    moe_gain, router_w, expert_ids, text_lengths, expert_in, expert_out,
):
    return call(
        enc_context, enc_out_w, enc_resid, final_gain, kv_weight, router_w.T, expert_ids.T, img_queries, img_resid,
        moe_gain, text_lengths, dec_out_w, expert_in[0], expert_out[0],
    )


def solution(mesh):
    placed = (
        P("dp", "mp"),
        P("dp", "mp"),
        P("mp", None),
        P("mp"),
        P(None, None, "mp"),
        P("dp", "mp"),
        P("dp", "mp"),
        P("mp", None),
        P("mp"),
        P("mp", None),
        P("dp", None),
        P("dp"),
        P("dp", None, "mp"),
        P("dp", "mp", None),
    )
    return jax.shard_map(
        local, mesh=mesh, in_specs=placed, out_specs=(P("dp", "mp"), P("dp", "mp")), check_vma=False
    )
```

```python
import functools
import jax
import jax.numpy as jnp
from jax import lax
from jax.experimental import pallas as pl
from jax.experimental.pallas import tpu as pltpu
from jax.sharding import PartitionSpec as P

HD = 64
EPSILON = 1e-06
SCORE_SCALE = 0.125
MESH = pl.DeviceIdType.MESH
NZ, NY, NX = 8, 4, 4
N_DP, N_MP = NZ * NY, NX * 2
EXPERTS = 32
WIDTH = 4096
SLICE = WIDTH // N_MP
ROWS = 128
FF_SLICE = 256
MSG_ROWS, MSG_LANES, CAP = 16, 768, 24
HALF = SLICE // 2
CHUNKS = 16
PER = N_DP // CHUNKS
F32, BF16 = jnp.float32, jnp.bfloat16
VMEM_LIMIT = 56 * 2**20


def remote(src, dst, send, recv, device):
    return pltpu.make_async_remote_copy(
        src_ref=src, dst_ref=dst, send_sem=send, recv_sem=recv, device_id=device, device_id_type=MESH
    )


def offset_of(order):
    turn, place = order // 4, order % 4
    kind, odd = turn % 2, place % 2
    reach = 1 + kind + 2 * (place // 2)
    dz = ((1 - odd) * reach + odd * (NZ - reach)) * (1 - kind * (place // 3))
    return dz, turn // 2


SPREAD = FF_SLICE // 2
PARTS = 2
PART = ROWS // PARTS
STATS = 40
AHEAD = 6
SELF = 7
LAGS = (0, 3, 4, 7, 10, 11, 14)


def kernel(*refs):
    sources, rest = refs[:14], refs[14:]
    (
        encoded, mixed,
        enc_context, enc_w, enc_resid, final_gain, kv_w, router, ids_row, img_queries, img_resid, moe_gain,
        lengths, dec_w, w_in, w_out,
        state, gathered, squares, tables, hidden, router_wide, picks, gated,
        enc_give, enc_kept, enc_taken, enc_sum_f, enc_sum_l, enc_sum_r,
        dec_give, dec_kept, dec_taken, dec_sum_f, dec_sum_l, dec_sum_r,
        packed, full, part_out, part_in, part_own, inner, last_out, last_in, last_own, done, back,
        load_sem, enc_send, enc_recv, dec_send, dec_recv, ag_send, ag_recv,
        square_send, square_recv, table_send, table_recv,
        disp_send, disp_recv, slot_send, slot_recv, inner_send, inner_recv, cross_send, cross_recv,
        in_send, in_recv, out_send, out_recv, ret_send, ret_recv,
    ) = rest
    targets = rest[2:16]
    dp, mp = lax.axis_index("dp"), lax.axis_index("mp")
    z, y = dp // NY, dp % NY
    x, core = mp // 2, mp % 2
    x_right, x_left, x_far = (x + 1) % NX, (x + NX - 1) % NX, (x + 2) % NX
    m_right, m_left, m_far = x_right * 2 + core, x_left * 2 + core, x_far * 2 + core
    sibling, right, left, far = (dp, x * 2 + 1 - core), (dp, m_right), (dp, m_left), (dp, m_far)

    def dest_of(order):
        dz, dy = offset_of(order)
        return ((z + dz) % NZ) * NY + (y + dy) % NY

    def origin_of(order):
        dz, dy = offset_of(order)
        return ((z + NZ - dz) % NZ) * NY + (y + NY - dy) % NY

    loads = [
        pltpu.make_async_copy(src, dst, load_sem.at[i])
        for i, (src, dst) in enumerate(zip(sources[:-2], targets))
    ]
    w_in_hbm, w_out_hbm = sources[-2:]

    x_a, x_b = NX - 1 - x, x + 1 - 2 * (x % 2)
    m_a, m_b, m_sib = x_a * 2 + core, x_b * 2 + core, x * 2 + 1 - core
    m_a_sib = x_a * 2 + 1 - core
    pair_a, pair_b = (dp, m_a), (dp, m_b)
    chip = 2 * SLICE

    def in_rows(of, start, count):
        return w_in_hbm.at[pl.ds(pl.multiple_of(of * chip + start, 128), count)]

    def out_block(part, m):
        return w_out_hbm.at[pl.ds(part * SPREAD, SPREAD), pl.ds(pl.multiple_of(m * SLICE, SLICE), SLICE)]

    def out_whole(m):
        return w_out_hbm.at[:, pl.ds(pl.multiple_of(m * SLICE, SLICE), SLICE)]

    count = len(sources)
    loads += [
        pltpu.make_async_copy(in_rows(x, 0, chip), w_in.at[0, pl.ds(0, chip)], load_sem.at[count - 2]),
        pltpu.make_async_copy(in_rows(x_a, 0, chip), w_in.at[0, pl.ds(chip, chip)], load_sem.at[count - 1]),
        pltpu.make_async_copy(out_whole(mp), w_out.at[0, 0], load_sem.at[count]),
        pltpu.make_async_copy(out_whole(m_b), w_out.at[0, 1], load_sem.at[count + 1]),
    ]

    def in_copy(piece):
        side, start = piece // 4, piece % 4 * FF_SLICE
        of = x_b if side == 0 else NX - 1 - x_b
        return remote(
            in_rows(of, start, FF_SLICE), w_in.at[1, pl.ds(side * chip + start, FF_SLICE)],
            in_send.at[piece], in_recv.at[piece], pair_b,
        )

    def out_copy(kind, piece):
        to = (m_sib, m_a, m_a_sib)[kind]
        which, part = piece // 2, piece % 2
        to_chip = to // 2
        m = to if which == 0 else (to_chip + 1 - 2 * (to_chip % 2)) * 2 + to % 2
        return remote(
            out_block(part, m), w_out.at[kind + 1, which, pl.ds(part * SPREAD, SPREAD)],
            out_send.at[kind, piece], out_recv.at[kind, piece], (dp, to),
        )

    def spread(ins, outs):
        for piece in ins:
            in_copy(piece).start()
        for unit in outs:
            out_copy(1 + unit % 2, unit // 2).start()

    for load in loads[:3]:
        load.start()
    barrier = pltpu.get_barrier_semaphore()
    for o in range(1, N_MP):
        pl.semaphore_signal(barrier, inc=1, device_id=(dp, (mp + o) % N_MP), device_id_type=MESH)

    def greet(order, carry):
        pl.semaphore_signal(barrier, inc=1, device_id=(dest_of(order), mp), device_id_type=MESH)
        return carry

    lax.fori_loop(0, SELF, greet, 0)
    lax.fori_loop(SELF + 1, N_DP, greet, 0)
    for load in loads[3:]:
        load.start()

    def reduce_scatter(values, weights, resid, out, give, kept, taken, sum_f, sum_l, sum_r, send, recv):
        def copy(kind, r):
            src, dst, device = {
                0: (give.at[r], taken.at[r], sibling),
                1: (kept.at[r, x_far], sum_f.at[r], far),
                2: (kept.at[r, x_right], sum_l.at[r], right),
                3: (kept.at[r, x_left], sum_r.at[r], left),
            }[kind]
            return remote(src, dst, send.at[kind, r], recv.at[kind, r], device)

        def product(ref, r, px, side):
            at = pl.multiple_of((px * 2 + side) * SLICE, SLICE)
            ref[r, px] = jnp.dot(
                values[r * PART:(r + 1) * PART], weights[:, pl.ds(at, SLICE)], preferred_element_type=F32
            ).astype(BF16)

        def pair(r, px, rows=slice(None)):
            return kept[r, px, rows].astype(F32) + taken[r, px, rows].astype(F32)

        for r in range(PARTS):
            for px in range(NX):
                product(give, r, px, 1 - core)
            if r == 0 and out is state:
                pl.semaphore_wait(barrier, N_MP - 1 + N_DP - 1)
            copy(0, r).start()
            if r == 0 and out is state:
                spread((0,), (0,))
                for piece in range(4):
                    out_copy(0, piece).start()
        for r in range(PARTS):
            for px in range(NX):
                product(kept, r, px, core)
        for r in range(PARTS):
            copy(0, r).wait_recv()
            for kind, px in ((1, x_far), (2, x_right), (3, x_left)):
                kept[r, px] = pair(r, px).astype(BF16)
                copy(kind, r).start()
        if out is state:
            pass
        else:
            pass
        for r in range(PARTS):
            rows = slice(r * PART, (r + 1) * PART)
            base = resid[rows].astype(F32) + pair(r, x)
            for kind in (2, 3, 1):
                copy(kind, r).wait_recv()
            out[rows] = base + sum_l[r].astype(F32) + sum_r[r].astype(F32) + sum_f[r].astype(F32)
            yield r

        def drain():
            for r in range(PARTS):
                for kind in range(4):
                    copy(kind, r).wait_send()

        drains.append(drain)

    drains = []

    def exchange(ref, send, recv):
        def copy(o):
            return remote(ref.at[mp], ref.at[mp], send.at[o], recv.at[mp], (dp, (mp + o) % N_MP))

        for o in range(1, N_MP):
            copy(o).start()

        def finish():
            for o in range(1, N_MP):
                other = ref.at[(mp + o) % N_MP]
                remote(other, other, send.at[o], recv.at[(mp + o) % N_MP], sibling).wait_recv()
            drains.append(lambda: [copy(o).wait_send() for o in range(1, N_MP)])

        return finish

    def gather_copy(kind):
        ref, device = {
            0: (gathered.at[mp, 0], sibling), 1: (gathered.at[mp, 1], sibling),
            2: (gathered.at[mp, 0], right), 3: (gathered.at[mp, 1], right),
            4: (gathered.at[mp, 0], left), 5: (gathered.at[mp, 1], left),
            6: (gathered.at[mp, 0], far), 7: (gathered.at[mp, 1], far),
            8: (gathered.at[m_left], sibling), 9: (gathered.at[m_right], sibling),
            10: (gathered.at[m_far], sibling),
        }[kind]
        return remote(ref, ref, ag_send.at[kind], ag_recv.at[kind], device)

    for load in loads[:4]:
        load.wait()
    text_gain = final_gain[...].astype(F32).reshape(1, SLICE)
    for r in reduce_scatter(
        enc_context[...], enc_w, enc_resid, state, enc_give, enc_kept, enc_taken, enc_sum_f,
        enc_sum_l, enc_sum_r, enc_send, enc_recv,
    ):
        gathered[mp, r] = (state[r * PART:(r + 1) * PART] * text_gain).astype(BF16)
        for kind in ((6, 2, 4, 0), (7, 3, 5, 1))[r]:
            gather_copy(kind).start()
    pass
    text_state = state[...]
    square = jnp.sum(text_state * text_state, axis=1, keepdims=True)
    squares[mp] = jnp.transpose(jnp.broadcast_to(square, (ROWS, ROWS)))[0:8]
    squares_done = exchange(squares, square_send, square_recv)

    for load in loads[4:]:
        load.wait()
    row_at = lax.broadcasted_iota(jnp.int32, (ROWS, ROWS), 0)
    col_at = lax.broadcasted_iota(jnp.int32, (ROWS, ROWS), 1)
    expert_row = lax.broadcasted_iota(jnp.int32, (EXPERTS, ROWS), 0)
    named_row = [jnp.where(expert_row == ids_row[k:k + 1, :], 1.0, 0.0) for k in range(2)]
    earlier_row = jnp.dot(
        (named_row[0] + named_row[1]).astype(BF16),
        jnp.where(row_at < col_at, 1.0, 0.0).astype(BF16),
        preferred_element_type=F32,
    )
    message = lax.broadcasted_iota(jnp.int32, (EXPERTS * MSG_ROWS, ROWS), 0)
    upper = (message // 8) % 2
    pick_head = jnp.zeros((EXPERTS * MSG_ROWS, ROWS), F32)
    pick_tail = jnp.zeros((EXPERTS * MSG_ROWS, ROWS), F32)
    slots = []
    for k in range(2):
        slot = jnp.sum(named_row[k] * earlier_row, axis=0, keepdims=True).astype(jnp.int32)
        slots.append(slot.astype(F32))
        base = ids_row[k:k + 1, :] * MSG_ROWS
        head_at = jnp.where(slot < MSG_ROWS, base + slot, -1)
        tail_at = jnp.where(slot >= MSG_ROWS, base + slot - MSG_ROWS, -1)
        pick_head = pick_head + jnp.where(message == head_at, 1.0, 0.0)
        pick_tail = pick_tail + jnp.where(message - 8 * upper == tail_at, 1.0, 0.0)
    picks[0] = pick_head.astype(BF16)
    picks[1] = pick_tail.astype(BF16)
    columns = jnp.transpose(
        jnp.concatenate([ids_row[...].astype(F32)] + slots + [jnp.zeros((ROWS - 4, ROWS), F32)], axis=0)
    )
    id_cols = [columns[:, k:k + 1].astype(jnp.int32) for k in range(2)]
    slot_cols = [columns[:, 2 + k:3 + k].astype(jnp.int32) for k in range(2)]
    router_wide[...] = jnp.zeros(router_wide.shape, F32)
    router_wide[0:EXPERTS] = router[...].astype(F32)

    sums = [jnp.zeros((ROWS, FF_SLICE), F32) for _ in range(2)]

    def project(m):
        at = pl.multiple_of(m * SLICE, SLICE)
        block = gathered[m].reshape(ROWS, SLICE)
        for which in range(2):
            sums[which] = sums[which] + jnp.dot(
                block, kv_w[which, pl.ds(at, SLICE), :], preferred_element_type=F32
            )

    project(mp)
    for kinds, on in (((2, 3), 8), ((4, 5), 9), ((6, 7), 10)):
        for kind in kinds:
            gather_copy(kind).wait_recv()
        gather_copy(on).start()
    spread((1, 2, 3, 4), (1, 2, 3, 4))
    project(m_left)
    project(m_right)
    gather_copy(0).wait_recv()
    gather_copy(1).wait_recv()
    project(x * 2 + 1 - core)
    project(m_far)
    for kind, px in ((8, x_left), (9, x_right), (10, x_far)):
        gather_copy(kind).wait_recv()
        project(px * 2 + 1 - core)
    squares_done()
    total = squares[0]
    for m in range(1, N_MP):
        total = total + squares[m]
    total = jnp.transpose(jnp.concatenate([total, jnp.zeros((ROWS - 8, ROWS), F32)], axis=0))[:, 0:1]
    text_scale = lax.rsqrt(total / WIDTH + EPSILON)
    encoded[...] = (state[...] * text_gain * text_scale).astype(BF16)
    keys = (sums[0] * text_scale).astype(BF16)
    values = (sums[1] * text_scale).astype(BF16)

    heads = FF_SLICE // HD
    head_of = lax.broadcasted_iota(jnp.int32, (ROWS, FF_SLICE), 1) // HD
    queries = img_queries[...]
    alone = jnp.concatenate([jnp.where(head_of == h, queries, jnp.zeros_like(queries)) for h in range(heads)], axis=0)
    scores = SCORE_SCALE * lax.dot_general(
        alone, keys, (((1,), (1,)), ((), ())), preferred_element_type=F32
    )
    valid = lax.broadcasted_iota(jnp.int32, scores.shape, 1) < lengths[0]
    scores = jnp.where(valid, scores, -jnp.inf)
    raised = jnp.exp(scores - jnp.max(scores, axis=1, keepdims=True))
    probs = (raised / jnp.sum(raised, axis=1, keepdims=True)).astype(BF16)
    mixed_heads = jnp.dot(probs, values, preferred_element_type=F32)
    context = jnp.zeros((ROWS, FF_SLICE), F32)
    for h in range(heads):
        context = context + jnp.where(head_of == h, mixed_heads[h * ROWS:(h + 1) * ROWS], 0.0)
    context = context.astype(BF16)

    for _ in reduce_scatter(
        context, dec_w, img_resid, hidden, dec_give, dec_kept, dec_taken, dec_sum_f,
        dec_sum_l, dec_sum_r, dec_send, dec_recv,
    ):
        pass
    here = hidden[...]
    gained = here * moe_gain[...].astype(F32).reshape(1, SLICE)
    square = jnp.sum(here * here, axis=1, keepdims=True)
    logits = lax.dot_general(
        gained, router_wide[...], (((1,), (1,)), ((), ())),
        precision=lax.Precision.HIGHEST, preferred_element_type=F32,
    )
    lane = lax.broadcasted_iota(jnp.int32, (ROWS, ROWS), 1)
    tables[mp] = jnp.transpose(jnp.where(lane == EXPERTS, square, logits))[0:STATS]
    tables_done = exchange(tables, table_send, table_recv)
    spread((5, 6, 7), (5, 6, 7))
    tables_done()
    total = tables[0]
    for m in range(1, N_MP):
        total = total + tables[m]
    table = jnp.transpose(jnp.concatenate([total, jnp.zeros((ROWS - STATS, ROWS), F32)], axis=0))
    rms = lax.rsqrt(table[:, EXPERTS:EXPERTS + 1] / WIDTH + EPSILON)
    normed = (gained * rms).astype(BF16)
    head = jnp.dot(picks[0], normed, preferred_element_type=F32)
    packed[:, :, 0:SLICE] = head.astype(BF16).reshape(EXPERTS, MSG_ROWS, SLICE)
    tail = jnp.dot(picks[1], normed, preferred_element_type=F32)
    upper = (lax.broadcasted_iota(jnp.int32, (EXPERTS * MSG_ROWS, ROWS), 0) // 8) % 2
    tail = jnp.where(upper[:, 0:1] == 0, tail[:, 0:HALF], tail[:, HALF:SLICE])
    packed[:, :, SLICE:MSG_LANES] = tail.astype(BF16).reshape(EXPERTS, MSG_ROWS, HALF)


    own = pltpu.make_async_copy(packed.at[dp], full.at[mp, SELF // PER, SELF % PER], disp_recv.at[SELF // PER])
    own.start()

    def dispatch(order, carry):
        dest = dest_of(order)
        chunk, place = order // PER, order % PER
        remote(packed.at[dest], full.at[mp, chunk, place], disp_send, disp_recv.at[chunk], (dest, mp)).start()
        return carry

    lax.fori_loop(0, SELF, dispatch, 0)
    lax.fori_loop(SELF + 1, AHEAD * PER, dispatch, 0)

    expert_col = lax.broadcasted_iota(jnp.int32, (ROWS, EXPERTS), 1)
    named_col = [jnp.where(expert_col == id_cols[k], 1.0, 0.0) for k in range(2)]
    logits = [rms * jnp.sum(named_col[k] * table[:, 0:EXPERTS], axis=1, keepdims=True) for k in range(2)]
    top = jnp.maximum(logits[0], logits[1])
    raised = [jnp.exp(value - top) for value in logits]
    place = lax.broadcasted_iota(jnp.int32, (ROWS, EXPERTS * MSG_ROWS), 1)
    gate_head = jnp.zeros(place.shape, F32)
    gate_low = jnp.zeros(place.shape, F32)
    gate_high = jnp.zeros(place.shape, F32)
    for k in range(2):
        gate = raised[k] / (raised[0] + raised[1])
        slot = slot_cols[k]
        base = id_cols[k] * MSG_ROWS
        head_at = jnp.where(slot < MSG_ROWS, base + slot, -1)
        tail_at = jnp.where(slot >= MSG_ROWS, base + slot - MSG_ROWS, -100)
        gate_head = gate_head + jnp.where(place == head_at, gate, 0.0)
        gate_low = gate_low + jnp.where(place == tail_at, gate, 0.0)
        gate_high = gate_high + jnp.where(place == tail_at + 8, gate, 0.0)

    for i, weights in enumerate((gate_head, gate_low, gate_high)):
        main = weights.astype(BF16)
        gated[2 * i] = main
        gated[2 * i + 1] = (weights - main.astype(F32)).astype(BF16)

    def shared_copy(ref, send, recv, kind, k):
        place, device = ((mp, sibling), (mp, pair_a), (m_a, sibling))[kind]
        return remote(ref.at[place, k], ref.at[place, k], send.at[kind, k], recv.at[kind, k], device)

    slot_copy = functools.partial(shared_copy, full, slot_send, slot_recv)
    inner_copy = functools.partial(shared_copy, inner, inner_send, inner_recv)

    def cross_copy(kind, k):
        src, dst = ((part_out, part_in), (last_out, last_in))[kind]
        return remote(src.at[k], dst.at[k], cross_send.at[kind, k], cross_recv.at[kind, k], pair_b)

    def arrive(k):
        @pl.when(k + AHEAD < CHUNKS)
        def _():
            first = (k + AHEAD) * PER
            lax.fori_loop(first, first + PER, dispatch, 0)

        pltpu.make_async_copy(full.at[mp, k], full.at[mp, k], disp_recv.at[k]).wait()
        for kind in (1, 0):
            slot_copy(kind, k).start()

    def forward(copy, k):
        copy(1, k).wait_recv()
        copy(2, k).start()

    rows = PER * MSG_ROWS

    def first_product(k):
        @pl.when(k == 0)
        def _():
            for piece in range(8):
                in_copy(piece).wait_recv()

        slot_copy(0, k).wait_recv()
        slot_copy(2, k).wait_recv()
        order = (x * 2, x * 2 + 1, x_a * 2, x_a * 2 + 1)

        def product(side):
            low = jnp.zeros((2 * rows, FF_SLICE), F32)
            high = jnp.zeros((2 * rows, FF_SLICE), F32)
            for j, m in enumerate(order):
                block = full[m, k].reshape(rows, MSG_LANES)
                end = block[:, SLICE:]
                low = low + jnp.dot(
                    jnp.concatenate([block[:, 0:HALF], end], axis=0),
                    w_in[side, j * SLICE:j * SLICE + HALF],
                    preferred_element_type=F32,
                )
                high = high + jnp.dot(
                    jnp.concatenate([block[:, HALF:SLICE], end], axis=0),
                    w_in[side, j * SLICE + HALF:(j + 1) * SLICE],
                    preferred_element_type=F32,
                )
            ends = (
                low[rows:].reshape(PER, MSG_ROWS, FF_SLICE)[:, 0:8]
                + high[rows:].reshape(PER, MSG_ROWS, FF_SLICE)[:, 8:16]
            )
            return jnp.concatenate([low[:rows] + high[:rows], ends.reshape(PER * 8, FF_SLICE)], axis=0)

        part_out[k] = product(1).astype(BF16)
        cross_copy(0, k).start()
        part_own[k] = product(0)

    def activate(k):
        cross_copy(0, k).wait_recv()
        before = part_own[k] + part_in[k].astype(F32)
        inner[mp, k] = jax.nn.gelu(before, approximate=True).astype(BF16)
        for kind in (1, 0):
            inner_copy(kind, k).start()

    def second_product(k):
        @pl.when(k == 0)
        def _():
            for kind in range(3):
                for piece in range(4):
                    out_copy(kind, piece).wait_recv()

        inner_copy(0, k).wait_recv()
        inner_copy(2, k).wait_recv()

        def product(ref, which):
            out = jnp.zeros((PER * CAP, SLICE), F32)
            for j, m in enumerate((mp, m_sib, m_a, m_a_sib)):
                out = out + jnp.dot(inner[m, k], w_out[j, which], preferred_element_type=F32)
            ref[k, :, :, 0:SLICE] = out[:rows].astype(ref.dtype).reshape(PER, MSG_ROWS, SLICE)
            ends = out[rows:].reshape(PER, 8, SLICE)
            ends = jnp.concatenate([ends[:, :, 0:HALF], ends[:, :, HALF:SLICE]], axis=1)
            ref[k, :, :, SLICE:MSG_LANES] = ends.astype(ref.dtype)

        product(last_out, 1)
        cross_copy(1, k).start()
        product(last_own, 0)

    def finish(k):
        cross_copy(1, k).wait_recv()
        done[k] = (last_own[k] + last_in[k].astype(F32)).astype(BF16)
        for j in range(PER):
            order = k * PER + j
            origin = origin_of(order)
            if j == SELF % PER:
                @pl.when(order == SELF)
                def _():
                    pltpu.make_async_copy(done.at[k, j], back.at[dp], ret_recv).start()

                @pl.when(order != SELF)
                def _():
                    remote(done.at[k, j], back.at[dp], ret_send, ret_recv, (origin, mp)).start()
            else:
                remote(done.at[k, j], back.at[dp], ret_send, ret_recv, (origin, mp)).start()
        for kind in range(3):
            slot_copy(kind, k).wait_send()
            inner_copy(kind, k).wait_send()
        for kind in range(2):
            cross_copy(kind, k).wait_send()

    stages = (
        arrive, functools.partial(forward, slot_copy), first_product, activate,
        functools.partial(forward, inner_copy), second_product, finish,
    )

    def step(i, carry):
        for lag, stage in zip(LAGS, stages):
            @pl.when((i >= lag) & (i - lag < CHUNKS))
            def _():
                stage(i - lag)
        return carry

    lax.fori_loop(0, CHUNKS + LAGS[-1], step, 0)

    pltpu.make_async_copy(back, back, ret_recv).wait()

    def weigh(i, values):
        return jnp.dot(gated[2 * i], values, preferred_element_type=F32) + jnp.dot(
            gated[2 * i + 1], values, preferred_element_type=F32
        )

    results = back[...].reshape(EXPERTS * MSG_ROWS, MSG_LANES)
    ends = results[:, SLICE:]
    moe = weigh(0, results[:, 0:SLICE])
    mixed[:, 0:HALF] = (hidden[:, 0:HALF] + moe[:, 0:HALF] + weigh(1, ends)).astype(BF16)
    mixed[:, HALF:] = (hidden[:, HALF:] + moe[:, HALF:] + weigh(2, ends)).astype(BF16)

    most = packed.at[pl.ds(0, N_DP - 1)]
    remote(most, most, disp_send, disp_recv.at[0], sibling).wait_send()
    remote(most, most, ret_send, ret_recv, sibling).wait_send()


    for drain in drains:
        drain()
    for kind in range(11):
        gather_copy(kind).wait_send()
    for piece in range(8):
        in_copy(piece).wait_send()
    for kind in range(3):
        for piece in range(4):
            out_copy(kind, piece).wait_send()


def call(*operands):
    vmem = pl.BlockSpec(memory_space=pltpu.VMEM)
    hbm = pl.BlockSpec(memory_space=pltpu.HBM)
    dma = pltpu.SemaphoreType.DMA
    block = (PER, MSG_ROWS, MSG_LANES)
    sums = [
        pltpu.VMEM((PARTS, NX, PART, SLICE), BF16),
        pltpu.VMEM((PARTS, NX, PART, SLICE), BF16),
        pltpu.VMEM((PARTS, NX, PART, SLICE), BF16),
        pltpu.VMEM((PARTS, PART, SLICE), BF16),
        pltpu.VMEM((PARTS, PART, SLICE), BF16),
        pltpu.VMEM((PARTS, PART, SLICE), BF16),
    ]
    landing = [
        pltpu.SMEM(o.shape, o.dtype) if o.shape == (1,) else pltpu.VMEM(o.shape, o.dtype) for o in operands[:-2]
    ] + [pltpu.VMEM((2, WIDTH // 2, FF_SLICE), BF16), pltpu.VMEM((4, 2, FF_SLICE, SLICE), BF16)]
    return pl.pallas_call(
        kernel,
        out_shape=(jax.ShapeDtypeStruct((ROWS, SLICE), BF16), jax.ShapeDtypeStruct((ROWS, SLICE), BF16)),
        in_specs=[hbm] * len(operands),
        out_specs=(vmem, vmem),
        scratch_shapes=landing + [
            pltpu.VMEM((ROWS, SLICE), F32),
            pltpu.VMEM((N_MP, PARTS, PART, SLICE), BF16),
            pltpu.VMEM((N_MP, 8, ROWS), F32),
            pltpu.VMEM((N_MP, STATS, ROWS), F32),
            pltpu.VMEM((ROWS, SLICE), F32),
            pltpu.VMEM((ROWS, SLICE), F32),
            pltpu.VMEM((2, EXPERTS * MSG_ROWS, ROWS), BF16),
            pltpu.VMEM((6, ROWS, EXPERTS * MSG_ROWS), BF16),
        ] + sums + sums + [
            pltpu.VMEM((EXPERTS, MSG_ROWS, MSG_LANES), BF16),
            pltpu.VMEM((N_MP, CHUNKS) + block, BF16),
            pltpu.VMEM((CHUNKS, PER * CAP, FF_SLICE), BF16),
            pltpu.VMEM((CHUNKS, PER * CAP, FF_SLICE), BF16),
            pltpu.VMEM((CHUNKS, PER * CAP, FF_SLICE), F32),
            pltpu.VMEM((N_MP, CHUNKS, PER * CAP, FF_SLICE), BF16),
            pltpu.VMEM((CHUNKS,) + block, BF16),
            pltpu.VMEM((CHUNKS,) + block, BF16),
            pltpu.VMEM((CHUNKS,) + block, F32),
            pltpu.VMEM((CHUNKS,) + block, BF16),
            pltpu.VMEM((EXPERTS, MSG_ROWS, MSG_LANES), BF16),
            dma((len(operands) + 2,)),
            dma((5, PARTS)),
            dma((5, PARTS)),
            dma((5, PARTS)),
            dma((5, PARTS)),
            dma((11,)),
            dma((11,)),
            dma((N_MP,)),
            dma((N_MP,)),
            dma((N_MP,)),
            dma((N_MP,)),
            dma,
            dma((CHUNKS,)),
            dma((3, CHUNKS)),
            dma((3, CHUNKS)),
            dma((3, CHUNKS)),
            dma((3, CHUNKS)),
            dma((2, CHUNKS)),
            dma((2, CHUNKS)),
            dma((8,)),
            dma((8,)),
            dma((3, 4)),
            dma((3, 4)),
            dma,
            dma,
        ],
        compiler_params=pltpu.CompilerParams(
            collective_id=1, has_side_effects=True, vmem_limit_bytes=VMEM_LIMIT
        ),
        name="whole",
    )(*operands)


def local(
    enc_context, enc_resid, enc_out_w, final_gain, kv_weight, img_queries, img_resid, dec_out_w,
    moe_gain, router_w, expert_ids, text_lengths, expert_in, expert_out,
):
    return call(
        enc_context, enc_out_w, enc_resid, final_gain, kv_weight, router_w.T, expert_ids.T, img_queries, img_resid,
        moe_gain, text_lengths, dec_out_w, expert_in[0], expert_out[0],
    )


def solution(mesh):
    placed = (
        P("dp", "mp"),
        P("dp", "mp"),
        P("mp", None),
        P("mp"),
        P(None, None, "mp"),
        P("dp", "mp"),
        P("dp", "mp"),
        P("mp", None),
        P("mp"),
        P("mp", None),
        P("dp", None),
        P("dp"),
        P("dp", None, "mp"),
        P("dp", "mp", None),
    )
    return jax.shard_map(
        local, mesh=mesh, in_specs=placed, out_specs=(P("dp", "mp"), P("dp", "mp")), check_vma=False
    )
```

```python
import functools
import jax
import jax.numpy as jnp
from jax import lax
from jax.experimental import pallas as pl
from jax.experimental.pallas import tpu as pltpu
from jax.sharding import PartitionSpec as P

HD = 64
EPSILON = 1e-06
SCORE_SCALE = 0.125
MESH = pl.DeviceIdType.MESH
NZ, NY, NX = 8, 4, 4
N_DP, N_MP = NZ * NY, NX * 2
EXPERTS = 32
WIDTH = 4096
SLICE = WIDTH // N_MP
ROWS = 128
FF_SLICE = 256
MSG_ROWS, MSG_LANES, CAP = 16, 768, 24
HALF = SLICE // 2
CHUNKS = 16
PER = N_DP // CHUNKS
F32, BF16 = jnp.float32, jnp.bfloat16
VMEM_LIMIT = 56 * 2**20


def remote(src, dst, send, recv, device):
    return pltpu.make_async_remote_copy(
        src_ref=src, dst_ref=dst, send_sem=send, recv_sem=recv, device_id=device, device_id_type=MESH
    )


def offset_of(order):
    high, place = order // 16, order % 8
    place = (1 - high) * place + high * (7 - place)
    kind, place = place // 4, place % 4
    odd = place % 2
    reach = 1 + kind + 2 * (place // 2)
    dz = ((1 - odd) * reach + odd * (NZ - reach)) * (1 - kind * (place // 3))
    return dz, order // 8


SPREAD = FF_SLICE // 2
PARTS = 2
PART = ROWS // PARTS
STATS = 40
AHEAD = 6
SELF = 7
LAGS = (0, 3, 4, 6, 9, 10, 13)


def kernel(*refs):
    sources, rest = refs[:14], refs[14:]
    (
        encoded, mixed,
        enc_context, enc_w, enc_resid, final_gain, kv_w, router, ids_row, img_queries, img_resid, moe_gain,
        lengths, dec_w, w_in, w_out,
        state, gathered, squares, tables, hidden, router_wide, picks, gated,
        enc_give, enc_kept, enc_taken, enc_sum_f, enc_sum_l, enc_sum_r,
        dec_give, dec_kept, dec_taken, dec_sum_f, dec_sum_l, dec_sum_r,
        packed, full, part_out, part_in, part_own, inner, last_out, last_in, last_own, done, back,
        load_sem, enc_send, enc_recv, dec_send, dec_recv, ag_send, ag_recv,
        square_send, square_recv, table_send, table_recv,
        disp_send, disp_recv, slot_send, slot_recv, inner_send, inner_recv, cross_send, cross_recv,
        in_send, in_recv, out_send, out_recv, ret_send, ret_recv,
    ) = rest
    targets = rest[2:16]
    dp, mp = lax.axis_index("dp"), lax.axis_index("mp")
    z, y = dp // NY, dp % NY
    x, core = mp // 2, mp % 2
    x_right, x_left, x_far = (x + 1) % NX, (x + NX - 1) % NX, (x + 2) % NX
    m_right, m_left, m_far = x_right * 2 + core, x_left * 2 + core, x_far * 2 + core
    sibling, right, left, far = (dp, x * 2 + 1 - core), (dp, m_right), (dp, m_left), (dp, m_far)

    def dest_of(order):
        dz, dy = offset_of(order)
        return ((z + dz) % NZ) * NY + (y + dy) % NY

    def origin_of(order):
        dz, dy = offset_of(order)
        return ((z + NZ - dz) % NZ) * NY + (y + NY - dy) % NY

    loads = [
        pltpu.make_async_copy(src, dst, load_sem.at[i])
        for i, (src, dst) in enumerate(zip(sources[:-2], targets))
    ]
    w_in_hbm, w_out_hbm = sources[-2:]

    x_a, x_b = NX - 1 - x, x + 1 - 2 * (x % 2)
    m_a, m_b, m_sib = x_a * 2 + core, x_b * 2 + core, x * 2 + 1 - core
    m_a_sib = x_a * 2 + 1 - core
    pair_a, pair_b = (dp, m_a), (dp, m_b)
    chip = 2 * SLICE

    def in_rows(of, start, count):
        return w_in_hbm.at[pl.ds(pl.multiple_of(of * chip + start, 128), count)]

    def out_block(part, m):
        return w_out_hbm.at[pl.ds(part * SPREAD, SPREAD), pl.ds(pl.multiple_of(m * SLICE, SLICE), SLICE)]

    def out_whole(m):
        return w_out_hbm.at[:, pl.ds(pl.multiple_of(m * SLICE, SLICE), SLICE)]

    count = len(sources)
    loads += [
        pltpu.make_async_copy(in_rows(x, 0, chip), w_in.at[0, pl.ds(0, chip)], load_sem.at[count - 2]),
        pltpu.make_async_copy(in_rows(x_a, 0, chip), w_in.at[0, pl.ds(chip, chip)], load_sem.at[count - 1]),
        pltpu.make_async_copy(out_whole(mp), w_out.at[0, 0], load_sem.at[count]),
        pltpu.make_async_copy(out_whole(m_b), w_out.at[0, 1], load_sem.at[count + 1]),
    ]

    def in_copy(piece):
        side, start = piece // 4, piece % 4 * FF_SLICE
        of = x_b if side == 0 else NX - 1 - x_b
        return remote(
            in_rows(of, start, FF_SLICE), w_in.at[1, pl.ds(side * chip + start, FF_SLICE)],
            in_send.at[piece], in_recv.at[piece], pair_b,
        )

    def out_copy(kind, piece):
        to = (m_sib, m_a, m_a_sib)[kind]
        which, part = piece // 2, piece % 2
        to_chip = to // 2
        m = to if which == 0 else (to_chip + 1 - 2 * (to_chip % 2)) * 2 + to % 2
        return remote(
            out_block(part, m), w_out.at[kind + 1, which, pl.ds(part * SPREAD, SPREAD)],
            out_send.at[kind, piece], out_recv.at[kind, piece], (dp, to),
        )

    def spread(ins, outs):
        for piece in ins:
            in_copy(piece).start()
        for unit in outs:
            out_copy(1 + unit % 2, unit // 2).start()

    for load in loads[:3]:
        load.start()
    barrier = pltpu.get_barrier_semaphore()
    for o in range(1, N_MP):
        pl.semaphore_signal(barrier, inc=1, device_id=(dp, (mp + o) % N_MP), device_id_type=MESH)

    def greet(order, carry):
        pl.semaphore_signal(barrier, inc=1, device_id=(dest_of(order), mp), device_id_type=MESH)
        return carry

    lax.fori_loop(0, SELF, greet, 0)
    lax.fori_loop(SELF + 1, N_DP, greet, 0)
    for load in loads[3:]:
        load.start()

    def reduce_scatter(values, weights, resid, out, give, kept, taken, sum_f, sum_l, sum_r, send, recv):
        def copy(kind, r):
            src, dst, device = {
                0: (give.at[r], taken.at[r], sibling),
                1: (kept.at[r, x_far], sum_f.at[r], far),
                2: (kept.at[r, x_right], sum_l.at[r], right),
                3: (kept.at[r, x_left], sum_r.at[r], left),
            }[kind]
            return remote(src, dst, send.at[kind, r], recv.at[kind, r], device)

        def product(ref, r, px, side):
            at = pl.multiple_of((px * 2 + side) * SLICE, SLICE)
            ref[r, px] = jnp.dot(
                values[r * PART:(r + 1) * PART], weights[:, pl.ds(at, SLICE)], preferred_element_type=F32
            ).astype(BF16)

        def pair(r, px, rows=slice(None)):
            return kept[r, px, rows].astype(F32) + taken[r, px, rows].astype(F32)

        for r in range(PARTS):
            for px in range(NX):
                product(give, r, px, 1 - core)
            if r == 0 and out is state:
                pl.semaphore_wait(barrier, N_MP - 1 + N_DP - 1)
            copy(0, r).start()
            if r == 0 and out is state:
                spread((0,), (0,))
                for piece in range(4):
                    out_copy(0, piece).start()
        for r in range(PARTS):
            for px in range(NX):
                product(kept, r, px, core)
        for r in range(PARTS):
            copy(0, r).wait_recv()
            for kind, px in ((1, x_far), (2, x_right), (3, x_left)):
                kept[r, px] = pair(r, px).astype(BF16)
                copy(kind, r).start()
        if out is state:
            pass
        else:
            pass
        for r in range(PARTS):
            rows = slice(r * PART, (r + 1) * PART)
            base = resid[rows].astype(F32) + pair(r, x)
            for kind in (2, 3, 1):
                copy(kind, r).wait_recv()
            out[rows] = base + sum_l[r].astype(F32) + sum_r[r].astype(F32) + sum_f[r].astype(F32)
            yield r

        def drain():
            for r in range(PARTS):
                for kind in range(4):
                    copy(kind, r).wait_send()

        drains.append(drain)

    drains = []

    def exchange(ref, send, recv):
        def copy(o):
            return remote(ref.at[mp], ref.at[mp], send.at[o], recv.at[mp], (dp, (mp + o) % N_MP))

        for o in range(1, N_MP):
            copy(o).start()

        def finish():
            for o in range(1, N_MP):
                other = ref.at[(mp + o) % N_MP]
                remote(other, other, send.at[o], recv.at[(mp + o) % N_MP], sibling).wait_recv()
            drains.append(lambda: [copy(o).wait_send() for o in range(1, N_MP)])

        return finish

    def gather_copy(kind):
        ref, device = {
            0: (gathered.at[mp, 0], sibling), 1: (gathered.at[mp, 1], sibling),
            2: (gathered.at[mp, 0], right), 3: (gathered.at[mp, 1], right),
            4: (gathered.at[mp, 0], left), 5: (gathered.at[mp, 1], left),
            6: (gathered.at[mp, 0], far), 7: (gathered.at[mp, 1], far),
            8: (gathered.at[m_left], sibling), 9: (gathered.at[m_right], sibling),
            10: (gathered.at[m_far], sibling),
        }[kind]
        return remote(ref, ref, ag_send.at[kind], ag_recv.at[kind], device)

    for load in loads[:4]:
        load.wait()
    text_gain = final_gain[...].astype(F32).reshape(1, SLICE)
    for r in reduce_scatter(
        enc_context[...], enc_w, enc_resid, state, enc_give, enc_kept, enc_taken, enc_sum_f,
        enc_sum_l, enc_sum_r, enc_send, enc_recv,
    ):
        gathered[mp, r] = (state[r * PART:(r + 1) * PART] * text_gain).astype(BF16)
        for kind in ((6, 2, 4, 0), (7, 3, 5, 1))[r]:
            gather_copy(kind).start()
    pass
    text_state = state[...]
    square = jnp.sum(text_state * text_state, axis=1, keepdims=True)
    squares[mp] = jnp.transpose(jnp.broadcast_to(square, (ROWS, ROWS)))[0:8]
    squares_done = exchange(squares, square_send, square_recv)

    for load in loads[4:]:
        load.wait()
    row_at = lax.broadcasted_iota(jnp.int32, (ROWS, ROWS), 0)
    col_at = lax.broadcasted_iota(jnp.int32, (ROWS, ROWS), 1)
    expert_row = lax.broadcasted_iota(jnp.int32, (EXPERTS, ROWS), 0)
    named_row = [jnp.where(expert_row == ids_row[k:k + 1, :], 1.0, 0.0) for k in range(2)]
    earlier_row = jnp.dot(
        (named_row[0] + named_row[1]).astype(BF16),
        jnp.where(row_at < col_at, 1.0, 0.0).astype(BF16),
        preferred_element_type=F32,
    )
    message = lax.broadcasted_iota(jnp.int32, (EXPERTS * MSG_ROWS, ROWS), 0)
    upper = (message // 8) % 2
    pick_head = jnp.zeros((EXPERTS * MSG_ROWS, ROWS), F32)
    pick_tail = jnp.zeros((EXPERTS * MSG_ROWS, ROWS), F32)
    slots = []
    for k in range(2):
        slot = jnp.sum(named_row[k] * earlier_row, axis=0, keepdims=True).astype(jnp.int32)
        slots.append(slot.astype(F32))
        base = ids_row[k:k + 1, :] * MSG_ROWS
        head_at = jnp.where(slot < MSG_ROWS, base + slot, -1)
        tail_at = jnp.where(slot >= MSG_ROWS, base + slot - MSG_ROWS, -1)
        pick_head = pick_head + jnp.where(message == head_at, 1.0, 0.0)
        pick_tail = pick_tail + jnp.where(message - 8 * upper == tail_at, 1.0, 0.0)
    picks[0] = pick_head.astype(BF16)
    picks[1] = pick_tail.astype(BF16)
    columns = jnp.transpose(
        jnp.concatenate([ids_row[...].astype(F32)] + slots + [jnp.zeros((ROWS - 4, ROWS), F32)], axis=0)
    )
    id_cols = [columns[:, k:k + 1].astype(jnp.int32) for k in range(2)]
    slot_cols = [columns[:, 2 + k:3 + k].astype(jnp.int32) for k in range(2)]
    router_wide[...] = jnp.zeros(router_wide.shape, F32)
    router_wide[0:EXPERTS] = router[...].astype(F32)

    sums = [jnp.zeros((ROWS, FF_SLICE), F32) for _ in range(2)]

    def project(m):
        at = pl.multiple_of(m * SLICE, SLICE)
        block = gathered[m].reshape(ROWS, SLICE)
        for which in range(2):
            sums[which] = sums[which] + jnp.dot(
                block, kv_w[which, pl.ds(at, SLICE), :], preferred_element_type=F32
            )

    project(mp)
    for kinds, on in (((2, 3), 8), ((4, 5), 9), ((6, 7), 10)):
        for kind in kinds:
            gather_copy(kind).wait_recv()
        gather_copy(on).start()
    spread((1, 2, 3), (1, 2, 3))
    project(m_left)
    project(m_right)
    gather_copy(0).wait_recv()
    gather_copy(1).wait_recv()
    project(x * 2 + 1 - core)
    project(m_far)
    for kind, px in ((8, x_left), (9, x_right), (10, x_far)):
        gather_copy(kind).wait_recv()
        project(px * 2 + 1 - core)
    squares_done()
    total = squares[0]
    for m in range(1, N_MP):
        total = total + squares[m]
    total = jnp.transpose(jnp.concatenate([total, jnp.zeros((ROWS - 8, ROWS), F32)], axis=0))[:, 0:1]
    text_scale = lax.rsqrt(total / WIDTH + EPSILON)
    encoded[...] = (state[...] * text_gain * text_scale).astype(BF16)
    keys = (sums[0] * text_scale).astype(BF16)
    values = (sums[1] * text_scale).astype(BF16)

    heads = FF_SLICE // HD
    head_of = lax.broadcasted_iota(jnp.int32, (ROWS, FF_SLICE), 1) // HD
    queries = img_queries[...]
    alone = jnp.concatenate([jnp.where(head_of == h, queries, jnp.zeros_like(queries)) for h in range(heads)], axis=0)
    scores = SCORE_SCALE * lax.dot_general(
        alone, keys, (((1,), (1,)), ((), ())), preferred_element_type=F32
    )
    valid = lax.broadcasted_iota(jnp.int32, scores.shape, 1) < lengths[0]
    scores = jnp.where(valid, scores, -jnp.inf)
    raised = jnp.exp(scores - jnp.max(scores, axis=1, keepdims=True))
    probs = (raised / jnp.sum(raised, axis=1, keepdims=True)).astype(BF16)
    mixed_heads = jnp.dot(probs, values, preferred_element_type=F32)
    context = jnp.zeros((ROWS, FF_SLICE), F32)
    for h in range(heads):
        context = context + jnp.where(head_of == h, mixed_heads[h * ROWS:(h + 1) * ROWS], 0.0)
    context = context.astype(BF16)

    for _ in reduce_scatter(
        context, dec_w, img_resid, hidden, dec_give, dec_kept, dec_taken, dec_sum_f,
        dec_sum_l, dec_sum_r, dec_send, dec_recv,
    ):
        pass
    here = hidden[...]
    gained = here * moe_gain[...].astype(F32).reshape(1, SLICE)
    square = jnp.sum(here * here, axis=1, keepdims=True)
    logits = lax.dot_general(
        gained, router_wide[...], (((1,), (1,)), ((), ())),
        precision=lax.Precision.HIGHEST, preferred_element_type=F32,
    )
    lane = lax.broadcasted_iota(jnp.int32, (ROWS, ROWS), 1)
    tables[mp] = jnp.transpose(jnp.where(lane == EXPERTS, square, logits))[0:STATS]
    tables_done = exchange(tables, table_send, table_recv)
    spread((4, 5, 6, 7), (4, 5, 6, 7))
    tables_done()
    total = tables[0]
    for m in range(1, N_MP):
        total = total + tables[m]
    table = jnp.transpose(jnp.concatenate([total, jnp.zeros((ROWS - STATS, ROWS), F32)], axis=0))
    rms = lax.rsqrt(table[:, EXPERTS:EXPERTS + 1] / WIDTH + EPSILON)
    normed = (gained * rms).astype(BF16)
    head = jnp.dot(picks[0], normed, preferred_element_type=F32)
    packed[:, :, 0:SLICE] = head.astype(BF16).reshape(EXPERTS, MSG_ROWS, SLICE)
    tail = jnp.dot(picks[1], normed, preferred_element_type=F32)
    upper = (lax.broadcasted_iota(jnp.int32, (EXPERTS * MSG_ROWS, ROWS), 0) // 8) % 2
    tail = jnp.where(upper[:, 0:1] == 0, tail[:, 0:HALF], tail[:, HALF:SLICE])
    packed[:, :, SLICE:MSG_LANES] = tail.astype(BF16).reshape(EXPERTS, MSG_ROWS, HALF)


    own = pltpu.make_async_copy(packed.at[dp], full.at[mp, SELF // PER, SELF % PER], disp_recv.at[SELF // PER])
    own.start()

    def dispatch(order, carry):
        dest = dest_of(order)
        chunk, place = order // PER, order % PER
        remote(packed.at[dest], full.at[mp, chunk, place], disp_send, disp_recv.at[chunk], (dest, mp)).start()
        return carry

    lax.fori_loop(0, SELF, dispatch, 0)
    lax.fori_loop(SELF + 1, AHEAD * PER, dispatch, 0)

    expert_col = lax.broadcasted_iota(jnp.int32, (ROWS, EXPERTS), 1)
    named_col = [jnp.where(expert_col == id_cols[k], 1.0, 0.0) for k in range(2)]
    logits = [rms * jnp.sum(named_col[k] * table[:, 0:EXPERTS], axis=1, keepdims=True) for k in range(2)]
    top = jnp.maximum(logits[0], logits[1])
    raised = [jnp.exp(value - top) for value in logits]
    place = lax.broadcasted_iota(jnp.int32, (ROWS, EXPERTS * MSG_ROWS), 1)
    gate_head = jnp.zeros(place.shape, F32)
    gate_low = jnp.zeros(place.shape, F32)
    gate_high = jnp.zeros(place.shape, F32)
    for k in range(2):
        gate = raised[k] / (raised[0] + raised[1])
        slot = slot_cols[k]
        base = id_cols[k] * MSG_ROWS
        head_at = jnp.where(slot < MSG_ROWS, base + slot, -1)
        tail_at = jnp.where(slot >= MSG_ROWS, base + slot - MSG_ROWS, -100)
        gate_head = gate_head + jnp.where(place == head_at, gate, 0.0)
        gate_low = gate_low + jnp.where(place == tail_at, gate, 0.0)
        gate_high = gate_high + jnp.where(place == tail_at + 8, gate, 0.0)

    for i, weights in enumerate((gate_head, gate_low, gate_high)):
        main = weights.astype(BF16)
        gated[2 * i] = main
        gated[2 * i + 1] = (weights - main.astype(F32)).astype(BF16)

    def shared_copy(ref, send, recv, kind, k):
        place, device = ((mp, sibling), (mp, pair_a), (m_a, sibling))[kind]
        return remote(ref.at[place, k], ref.at[place, k], send.at[kind, k], recv.at[kind, k], device)

    slot_copy = functools.partial(shared_copy, full, slot_send, slot_recv)
    inner_copy = functools.partial(shared_copy, inner, inner_send, inner_recv)

    def cross_copy(kind, k):
        src, dst = ((part_out, part_in), (last_out, last_in))[kind]
        return remote(src.at[k], dst.at[k], cross_send.at[kind, k], cross_recv.at[kind, k], pair_b)

    def arrive(k):
        @pl.when(k + AHEAD < CHUNKS)
        def _():
            first = (k + AHEAD) * PER
            lax.fori_loop(first, first + PER, dispatch, 0)

        pltpu.make_async_copy(full.at[mp, k], full.at[mp, k], disp_recv.at[k]).wait()
        for kind in (1, 0):
            slot_copy(kind, k).start()

    def forward(copy, k):
        copy(1, k).wait_recv()
        copy(2, k).start()

    rows = PER * MSG_ROWS

    def first_product(k):
        @pl.when(k == 0)
        def _():
            for piece in range(8):
                in_copy(piece).wait_recv()

        slot_copy(0, k).wait_recv()
        slot_copy(2, k).wait_recv()
        order = (x * 2, x * 2 + 1, x_a * 2, x_a * 2 + 1)

        def product(side):
            low = jnp.zeros((2 * rows, FF_SLICE), F32)
            high = jnp.zeros((2 * rows, FF_SLICE), F32)
            for j, m in enumerate(order):
                block = full[m, k].reshape(rows, MSG_LANES)
                end = block[:, SLICE:]
                low = low + jnp.dot(
                    jnp.concatenate([block[:, 0:HALF], end], axis=0),
                    w_in[side, j * SLICE:j * SLICE + HALF],
                    preferred_element_type=F32,
                )
                high = high + jnp.dot(
                    jnp.concatenate([block[:, HALF:SLICE], end], axis=0),
                    w_in[side, j * SLICE + HALF:(j + 1) * SLICE],
                    preferred_element_type=F32,
                )
            ends = (
                low[rows:].reshape(PER, MSG_ROWS, FF_SLICE)[:, 0:8]
                + high[rows:].reshape(PER, MSG_ROWS, FF_SLICE)[:, 8:16]
            )
            return jnp.concatenate([low[:rows] + high[:rows], ends.reshape(PER * 8, FF_SLICE)], axis=0)

        part_out[k] = product(1).astype(BF16)
        cross_copy(0, k).start()
        part_own[k] = product(0)

    def activate(k):
        cross_copy(0, k).wait_recv()
        before = part_own[k] + part_in[k].astype(F32)
        inner[mp, k] = jax.nn.gelu(before, approximate=True).astype(BF16)
        for kind in (1, 0):
            inner_copy(kind, k).start()

    def second_product(k):
        @pl.when(k == 0)
        def _():
            for kind in range(3):
                for piece in range(4):
                    out_copy(kind, piece).wait_recv()

        inner_copy(0, k).wait_recv()
        inner_copy(2, k).wait_recv()

        def product(ref, which):
            out = jnp.zeros((PER * CAP, SLICE), F32)
            for j, m in enumerate((mp, m_sib, m_a, m_a_sib)):
                out = out + jnp.dot(inner[m, k], w_out[j, which], preferred_element_type=F32)
            ref[k, :, :, 0:SLICE] = out[:rows].astype(ref.dtype).reshape(PER, MSG_ROWS, SLICE)
            ends = out[rows:].reshape(PER, 8, SLICE)
            ends = jnp.concatenate([ends[:, :, 0:HALF], ends[:, :, HALF:SLICE]], axis=1)
            ref[k, :, :, SLICE:MSG_LANES] = ends.astype(ref.dtype)

        product(last_out, 1)
        cross_copy(1, k).start()
        product(last_own, 0)

    def finish(k):
        cross_copy(1, k).wait_recv()
        done[k] = (last_own[k] + last_in[k].astype(F32)).astype(BF16)
        for j in range(PER):
            order = k * PER + j
            origin = origin_of(order)
            if j == SELF % PER:
                @pl.when(order == SELF)
                def _():
                    pltpu.make_async_copy(done.at[k, j], back.at[dp], ret_recv).start()

                @pl.when(order != SELF)
                def _():
                    remote(done.at[k, j], back.at[dp], ret_send, ret_recv, (origin, mp)).start()
            else:
                remote(done.at[k, j], back.at[dp], ret_send, ret_recv, (origin, mp)).start()
        for kind in range(3):
            slot_copy(kind, k).wait_send()
            inner_copy(kind, k).wait_send()
        for kind in range(2):
            cross_copy(kind, k).wait_send()

    stages = (
        arrive, functools.partial(forward, slot_copy), first_product, activate,
        functools.partial(forward, inner_copy), second_product, finish,
    )

    def step(i, carry):
        for lag, stage in zip(LAGS, stages):
            @pl.when((i >= lag) & (i - lag < CHUNKS))
            def _():
                stage(i - lag)
        return carry

    lax.fori_loop(0, CHUNKS + LAGS[-1], step, 0)

    for drain in drains:
        drain()
    for kind in range(11):
        gather_copy(kind).wait_send()
    for piece in range(8):
        in_copy(piece).wait_send()
    for kind in range(3):
        for piece in range(4):
            out_copy(kind, piece).wait_send()

    pltpu.make_async_copy(back, back, ret_recv).wait()

    def weigh(i, values):
        return jnp.dot(gated[2 * i], values, preferred_element_type=F32) + jnp.dot(
            gated[2 * i + 1], values, preferred_element_type=F32
        )

    results = back[...].reshape(EXPERTS * MSG_ROWS, MSG_LANES)
    ends = results[:, SLICE:]
    moe = weigh(0, results[:, 0:SLICE])
    mixed[:, 0:HALF] = (hidden[:, 0:HALF] + moe[:, 0:HALF] + weigh(1, ends)).astype(BF16)
    mixed[:, HALF:] = (hidden[:, HALF:] + moe[:, HALF:] + weigh(2, ends)).astype(BF16)

    most = packed.at[pl.ds(0, N_DP - 1)]
    remote(most, most, disp_send, disp_recv.at[0], sibling).wait_send()
    remote(most, most, ret_send, ret_recv, sibling).wait_send()


def call(*operands):
    vmem = pl.BlockSpec(memory_space=pltpu.VMEM)
    hbm = pl.BlockSpec(memory_space=pltpu.HBM)
    dma = pltpu.SemaphoreType.DMA
    block = (PER, MSG_ROWS, MSG_LANES)
    sums = [
        pltpu.VMEM((PARTS, NX, PART, SLICE), BF16),
        pltpu.VMEM((PARTS, NX, PART, SLICE), BF16),
        pltpu.VMEM((PARTS, NX, PART, SLICE), BF16),
        pltpu.VMEM((PARTS, PART, SLICE), BF16),
        pltpu.VMEM((PARTS, PART, SLICE), BF16),
        pltpu.VMEM((PARTS, PART, SLICE), BF16),
    ]
    landing = [
        pltpu.SMEM(o.shape, o.dtype) if o.shape == (1,) else pltpu.VMEM(o.shape, o.dtype) for o in operands[:-2]
    ] + [pltpu.VMEM((2, WIDTH // 2, FF_SLICE), BF16), pltpu.VMEM((4, 2, FF_SLICE, SLICE), BF16)]
    return pl.pallas_call(
        kernel,
        out_shape=(jax.ShapeDtypeStruct((ROWS, SLICE), BF16), jax.ShapeDtypeStruct((ROWS, SLICE), BF16)),
        in_specs=[hbm] * len(operands),
        out_specs=(vmem, vmem),
        scratch_shapes=landing + [
            pltpu.VMEM((ROWS, SLICE), F32),
            pltpu.VMEM((N_MP, PARTS, PART, SLICE), BF16),
            pltpu.VMEM((N_MP, 8, ROWS), F32),
            pltpu.VMEM((N_MP, STATS, ROWS), F32),
            pltpu.VMEM((ROWS, SLICE), F32),
            pltpu.VMEM((ROWS, SLICE), F32),
            pltpu.VMEM((2, EXPERTS * MSG_ROWS, ROWS), BF16),
            pltpu.VMEM((6, ROWS, EXPERTS * MSG_ROWS), BF16),
        ] + sums + sums + [
            pltpu.VMEM((EXPERTS, MSG_ROWS, MSG_LANES), BF16),
            pltpu.VMEM((N_MP, CHUNKS) + block, BF16),
            pltpu.VMEM((CHUNKS, PER * CAP, FF_SLICE), BF16),
            pltpu.VMEM((CHUNKS, PER * CAP, FF_SLICE), BF16),
            pltpu.VMEM((CHUNKS, PER * CAP, FF_SLICE), F32),
            pltpu.VMEM((N_MP, CHUNKS, PER * CAP, FF_SLICE), BF16),
            pltpu.VMEM((CHUNKS,) + block, BF16),
            pltpu.VMEM((CHUNKS,) + block, BF16),
            pltpu.VMEM((CHUNKS,) + block, F32),
            pltpu.VMEM((CHUNKS,) + block, BF16),
            pltpu.VMEM((EXPERTS, MSG_ROWS, MSG_LANES), BF16),
            dma((len(operands) + 2,)),
            dma((5, PARTS)),
            dma((5, PARTS)),
            dma((5, PARTS)),
            dma((5, PARTS)),
            dma((11,)),
            dma((11,)),
            dma((N_MP,)),
            dma((N_MP,)),
            dma((N_MP,)),
            dma((N_MP,)),
            dma,
            dma((CHUNKS,)),
            dma((3, CHUNKS)),
            dma((3, CHUNKS)),
            dma((3, CHUNKS)),
            dma((3, CHUNKS)),
            dma((2, CHUNKS)),
            dma((2, CHUNKS)),
            dma((8,)),
            dma((8,)),
            dma((3, 4)),
            dma((3, 4)),
            dma,
            dma,
        ],
        compiler_params=pltpu.CompilerParams(
            collective_id=1, has_side_effects=True, vmem_limit_bytes=VMEM_LIMIT
        ),
        name="whole",
    )(*operands)


def local(
    enc_context, enc_resid, enc_out_w, final_gain, kv_weight, img_queries, img_resid, dec_out_w,
    moe_gain, router_w, expert_ids, text_lengths, expert_in, expert_out,
):
    return call(
        enc_context, enc_out_w, enc_resid, final_gain, kv_weight, router_w.T, expert_ids.T, img_queries, img_resid,
        moe_gain, text_lengths, dec_out_w, expert_in[0], expert_out[0],
    )


def solution(mesh):
    placed = (
        P("dp", "mp"),
        P("dp", "mp"),
        P("mp", None),
        P("mp"),
        P(None, None, "mp"),
        P("dp", "mp"),
        P("dp", "mp"),
        P("mp", None),
        P("mp"),
        P("mp", None),
        P("dp", None),
        P("dp"),
        P("dp", None, "mp"),
        P("dp", "mp", None),
    )
    return jax.shard_map(
        local, mesh=mesh, in_specs=placed, out_specs=(P("dp", "mp"), P("dp", "mp")), check_vma=False
    )
```

```python
import functools
import jax
import jax.numpy as jnp
from jax import lax
from jax.experimental import pallas as pl
from jax.experimental.pallas import tpu as pltpu
from jax.sharding import PartitionSpec as P

HD = 64
EPSILON = 1e-06
SCORE_SCALE = 0.125
MESH = pl.DeviceIdType.MESH
NZ, NY, NX = 8, 4, 4
N_DP, N_MP = NZ * NY, NX * 2
EXPERTS = 32
WIDTH = 4096
SLICE = WIDTH // N_MP
ROWS = 128
FF_SLICE = 256
MSG_ROWS, MSG_LANES, CAP = 16, 768, 24
HALF = SLICE // 2
CHUNKS = 16
PER = N_DP // CHUNKS
F32, BF16 = jnp.float32, jnp.bfloat16
VMEM_LIMIT = 56 * 2**20


def remote(src, dst, send, recv, device):
    return pltpu.make_async_remote_copy(
        src_ref=src, dst_ref=dst, send_sem=send, recv_sem=recv, device_id=device, device_id_type=MESH
    )


def offset_of(order):
    high, place = order // 16, order % 8
    place = (1 - high) * place + high * (7 - place)
    kind, place = place // 4, place % 4
    odd = place % 2
    reach = 1 + kind + 2 * (place // 2)
    dz = ((1 - odd) * reach + odd * (NZ - reach)) * (1 - kind * (place // 3))
    return dz, order // 8


SPREAD = FF_SLICE // 2
PARTS = 2
PART = ROWS // PARTS
STATS = 40
AHEAD = 6
SELF = 7
LAGS = (0, 3, 4, 6, 9, 10, 13)


def kernel(*refs):
    sources, rest = refs[:14], refs[14:]
    (
        both,
        enc_context, enc_w, enc_resid, final_gain, kv_w, router, ids_row, img_queries, img_resid, moe_gain,
        lengths, dec_w, w_in, w_out,
        state, gathered, squares, tables, hidden, router_wide, picks, gated,
        enc_give, enc_kept, enc_taken, enc_sum_f, enc_sum_l, enc_sum_r,
        dec_give, dec_kept, dec_taken, dec_sum_f, dec_sum_l, dec_sum_r,
        packed, full, part_out, part_in, part_own, inner, last_out, last_in, last_own, done, back,
        load_sem, enc_send, enc_recv, dec_send, dec_recv, ag_send, ag_recv,
        square_send, square_recv, table_send, table_recv,
        disp_send, disp_recv, slot_send, slot_recv, inner_send, inner_recv, cross_send, cross_recv,
        in_send, in_recv, out_send, out_recv, ret_send, ret_recv,
    ) = rest
    targets = rest[1:15]
    encoded, mixed = both.at[0], both.at[1]
    dp, mp = lax.axis_index("dp"), lax.axis_index("mp")
    z, y = dp // NY, dp % NY
    x, core = mp // 2, mp % 2
    x_right, x_left, x_far = (x + 1) % NX, (x + NX - 1) % NX, (x + 2) % NX
    m_right, m_left, m_far = x_right * 2 + core, x_left * 2 + core, x_far * 2 + core
    sibling, right, left, far = (dp, x * 2 + 1 - core), (dp, m_right), (dp, m_left), (dp, m_far)

    def dest_of(order):
        dz, dy = offset_of(order)
        return ((z + dz) % NZ) * NY + (y + dy) % NY

    def origin_of(order):
        dz, dy = offset_of(order)
        return ((z + NZ - dz) % NZ) * NY + (y + NY - dy) % NY

    loads = [
        pltpu.make_async_copy(src, dst, load_sem.at[i])
        for i, (src, dst) in enumerate(zip(sources[:-2], targets))
    ]
    w_in_hbm, w_out_hbm = sources[-2:]

    x_a, x_b = NX - 1 - x, x + 1 - 2 * (x % 2)
    m_a, m_b, m_sib = x_a * 2 + core, x_b * 2 + core, x * 2 + 1 - core
    m_a_sib = x_a * 2 + 1 - core
    pair_a, pair_b = (dp, m_a), (dp, m_b)
    chip = 2 * SLICE

    def in_rows(of, start, count):
        return w_in_hbm.at[pl.ds(pl.multiple_of(of * chip + start, 128), count)]

    def out_block(part, m):
        return w_out_hbm.at[pl.ds(part * SPREAD, SPREAD), pl.ds(pl.multiple_of(m * SLICE, SLICE), SLICE)]

    def out_whole(m):
        return w_out_hbm.at[:, pl.ds(pl.multiple_of(m * SLICE, SLICE), SLICE)]

    count = len(sources)
    loads += [
        pltpu.make_async_copy(in_rows(x, 0, chip), w_in.at[0, pl.ds(0, chip)], load_sem.at[count - 2]),
        pltpu.make_async_copy(in_rows(x_a, 0, chip), w_in.at[0, pl.ds(chip, chip)], load_sem.at[count - 1]),
        pltpu.make_async_copy(out_whole(mp), w_out.at[0, 0], load_sem.at[count]),
        pltpu.make_async_copy(out_whole(m_b), w_out.at[0, 1], load_sem.at[count + 1]),
    ]

    def in_copy(piece):
        side, start = piece // 4, piece % 4 * FF_SLICE
        of = x_b if side == 0 else NX - 1 - x_b
        return remote(
            in_rows(of, start, FF_SLICE), w_in.at[1, pl.ds(side * chip + start, FF_SLICE)],
            in_send.at[piece], in_recv.at[piece], pair_b,
        )

    def out_copy(kind, piece):
        to = (m_sib, m_a, m_a_sib)[kind]
        which, part = piece // 2, piece % 2
        to_chip = to // 2
        m = to if which == 0 else (to_chip + 1 - 2 * (to_chip % 2)) * 2 + to % 2
        return remote(
            out_block(part, m), w_out.at[kind + 1, which, pl.ds(part * SPREAD, SPREAD)],
            out_send.at[kind, piece], out_recv.at[kind, piece], (dp, to),
        )

    def spread(ins, outs):
        for piece, unit in zip(ins, outs):
            in_copy(piece).start()
            out_copy(1 + unit % 2, unit // 2).start()

    for load in loads[:3]:
        load.start()
    barrier = pltpu.get_barrier_semaphore()
    for o in range(1, N_MP):
        pl.semaphore_signal(barrier, inc=1, device_id=(dp, (mp + o) % N_MP), device_id_type=MESH)

    def greet(order, carry):
        pl.semaphore_signal(barrier, inc=1, device_id=(dest_of(order), mp), device_id_type=MESH)
        return carry

    lax.fori_loop(0, SELF, greet, 0)
    lax.fori_loop(SELF + 1, N_DP, greet, 0)
    for load in loads[3:]:
        load.start()

    def reduce_scatter(values, weights, resid, out, give, kept, taken, sum_f, sum_l, sum_r, send, recv):
        def copy(kind, r):
            src, dst, device = {
                0: (give.at[r], taken.at[r], sibling),
                1: (kept.at[r, x_far], sum_f.at[r], far),
                2: (kept.at[r, x_right], sum_l.at[r], right),
                3: (kept.at[r, x_left], sum_r.at[r], left),
            }[kind]
            return remote(src, dst, send.at[kind, r], recv.at[kind, r], device)

        def product(ref, r, px, side):
            at = pl.multiple_of((px * 2 + side) * SLICE, SLICE)
            ref[r, px] = jnp.dot(
                values[r * PART:(r + 1) * PART], weights[:, pl.ds(at, SLICE)], preferred_element_type=F32
            ).astype(BF16)

        def pair(r, px, rows=slice(None)):
            return kept[r, px, rows].astype(F32) + taken[r, px, rows].astype(F32)

        for r in range(PARTS):
            for px in range(NX):
                product(give, r, px, 1 - core)
            if r == 0 and out is state:
                pl.semaphore_wait(barrier, N_MP - 1 + N_DP - 1)
            copy(0, r).start()
            if r == 0 and out is state:
                spread((0,), (0,))
                for piece in range(4):
                    out_copy(0, piece).start()
        for r in range(PARTS):
            for px in range(NX):
                product(kept, r, px, core)
        for r in range(PARTS):
            copy(0, r).wait_recv()
            for kind, px in ((1, x_far), (2, x_right), (3, x_left)):
                kept[r, px] = pair(r, px).astype(BF16)
                copy(kind, r).start()
        for r in range(PARTS):
            rows = slice(r * PART, (r + 1) * PART)
            base = resid[rows].astype(F32) + pair(r, x)
            for kind in (2, 3, 1):
                copy(kind, r).wait_recv()
            out[rows] = base + sum_l[r].astype(F32) + sum_r[r].astype(F32) + sum_f[r].astype(F32)
            yield r

        def drain():
            for r in range(PARTS):
                for kind in range(4):
                    copy(kind, r).wait_send()

        drains.append(drain)

    drains = []

    def exchange(ref, send, recv):
        def copy(o):
            return remote(ref.at[mp], ref.at[mp], send.at[o], recv.at[mp], (dp, (mp + o) % N_MP))

        for o in range(1, N_MP):
            copy(o).start()

        def finish():
            for o in range(1, N_MP):
                other = ref.at[(mp + o) % N_MP]
                remote(other, other, send.at[o], recv.at[(mp + o) % N_MP], sibling).wait_recv()
            drains.append(lambda: [copy(o).wait_send() for o in range(1, N_MP)])

        return finish

    def gather_copy(kind):
        ref, device = {
            0: (gathered.at[mp, 0], sibling), 1: (gathered.at[mp, 1], sibling),
            2: (gathered.at[mp, 0], right), 3: (gathered.at[mp, 1], right),
            4: (gathered.at[mp, 0], left), 5: (gathered.at[mp, 1], left),
            6: (gathered.at[mp, 0], far), 7: (gathered.at[mp, 1], far),
            8: (gathered.at[m_left], sibling), 9: (gathered.at[m_right], sibling),
            10: (gathered.at[m_far], sibling),
        }[kind]
        return remote(ref, ref, ag_send.at[kind], ag_recv.at[kind], device)

    for load in loads[:4]:
        load.wait()
    text_gain = final_gain[...].astype(F32).reshape(1, SLICE)
    for r in reduce_scatter(
        enc_context[...], enc_w, enc_resid, state, enc_give, enc_kept, enc_taken, enc_sum_f,
        enc_sum_l, enc_sum_r, enc_send, enc_recv,
    ):
        gathered[mp, r] = (state[r * PART:(r + 1) * PART] * text_gain).astype(BF16)
        for kind in ((6, 2, 4, 0), (7, 3, 5, 1))[r]:
            gather_copy(kind).start()
    text_state = state[...]
    square = jnp.sum(text_state * text_state, axis=1, keepdims=True)
    squares[mp] = jnp.transpose(jnp.broadcast_to(square, (ROWS, ROWS)))[0:8]
    squares_done = exchange(squares, square_send, square_recv)

    for load in loads[4:]:
        load.wait()
    row_at = lax.broadcasted_iota(jnp.int32, (ROWS, ROWS), 0)
    col_at = lax.broadcasted_iota(jnp.int32, (ROWS, ROWS), 1)
    expert_row = lax.broadcasted_iota(jnp.int32, (EXPERTS, ROWS), 0)
    named_row = [jnp.where(expert_row == ids_row[k:k + 1, :], 1.0, 0.0) for k in range(2)]
    earlier_row = jnp.dot(
        (named_row[0] + named_row[1]).astype(BF16),
        jnp.where(row_at < col_at, 1.0, 0.0).astype(BF16),
        preferred_element_type=F32,
    )
    message = lax.broadcasted_iota(jnp.int32, (EXPERTS * MSG_ROWS, ROWS), 0)
    upper = (message // 8) % 2
    pick_head = jnp.zeros((EXPERTS * MSG_ROWS, ROWS), F32)
    pick_tail = jnp.zeros((EXPERTS * MSG_ROWS, ROWS), F32)
    slots = []
    for k in range(2):
        slot = jnp.sum(named_row[k] * earlier_row, axis=0, keepdims=True).astype(jnp.int32)
        slots.append(slot.astype(F32))
        base = ids_row[k:k + 1, :] * MSG_ROWS
        head_at = jnp.where(slot < MSG_ROWS, base + slot, -1)
        tail_at = jnp.where(slot >= MSG_ROWS, base + slot - MSG_ROWS, -1)
        pick_head = pick_head + jnp.where(message == head_at, 1.0, 0.0)
        pick_tail = pick_tail + jnp.where(message - 8 * upper == tail_at, 1.0, 0.0)
    picks[0] = pick_head.astype(BF16)
    picks[1] = pick_tail.astype(BF16)
    columns = jnp.transpose(
        jnp.concatenate([ids_row[...].astype(F32)] + slots + [jnp.zeros((ROWS - 4, ROWS), F32)], axis=0)
    )
    id_cols = [columns[:, k:k + 1].astype(jnp.int32) for k in range(2)]
    slot_cols = [columns[:, 2 + k:3 + k].astype(jnp.int32) for k in range(2)]
    router_wide[...] = jnp.zeros(router_wide.shape, F32)
    router_wide[0:EXPERTS] = router[...].astype(F32)

    sums = [jnp.zeros((ROWS, FF_SLICE), F32) for _ in range(2)]

    def project(m):
        at = pl.multiple_of(m * SLICE, SLICE)
        block = gathered[m].reshape(ROWS, SLICE)
        for which in range(2):
            sums[which] = sums[which] + jnp.dot(
                block, kv_w[which, pl.ds(at, SLICE), :], preferred_element_type=F32
            )

    project(mp)
    for kinds, on in (((2, 3), 8), ((4, 5), 9), ((6, 7), 10)):
        for kind in kinds:
            gather_copy(kind).wait_recv()
        gather_copy(on).start()
    spread((1, 2, 3), (1, 2, 3))
    project(m_left)
    project(m_right)
    gather_copy(0).wait_recv()
    gather_copy(1).wait_recv()
    project(x * 2 + 1 - core)
    project(m_far)
    for kind, px in ((8, x_left), (9, x_right), (10, x_far)):
        gather_copy(kind).wait_recv()
        project(px * 2 + 1 - core)
    squares_done()
    total = squares[0]
    for m in range(1, N_MP):
        total = total + squares[m]
    total = jnp.transpose(jnp.concatenate([total, jnp.zeros((ROWS - 8, ROWS), F32)], axis=0))[:, 0:1]
    text_scale = lax.rsqrt(total / WIDTH + EPSILON)
    encoded[...] = (state[...] * text_gain * text_scale).astype(BF16)
    keys = (sums[0] * text_scale).astype(BF16)
    values = (sums[1] * text_scale).astype(BF16)

    heads = FF_SLICE // HD
    head_of = lax.broadcasted_iota(jnp.int32, (ROWS, FF_SLICE), 1) // HD
    queries = img_queries[...]
    alone = jnp.concatenate([jnp.where(head_of == h, queries, jnp.zeros_like(queries)) for h in range(heads)], axis=0)
    scores = SCORE_SCALE * lax.dot_general(
        alone, keys, (((1,), (1,)), ((), ())), preferred_element_type=F32
    )
    valid = lax.broadcasted_iota(jnp.int32, scores.shape, 1) < lengths[0]
    scores = jnp.where(valid, scores, -jnp.inf)
    raised = jnp.exp(scores - jnp.max(scores, axis=1, keepdims=True))
    probs = (raised / jnp.sum(raised, axis=1, keepdims=True)).astype(BF16)
    mixed_heads = jnp.dot(probs, values, preferred_element_type=F32)
    context = jnp.zeros((ROWS, FF_SLICE), F32)
    for h in range(heads):
        context = context + jnp.where(head_of == h, mixed_heads[h * ROWS:(h + 1) * ROWS], 0.0)
    context = context.astype(BF16)

    for _ in reduce_scatter(
        context, dec_w, img_resid, hidden, dec_give, dec_kept, dec_taken, dec_sum_f,
        dec_sum_l, dec_sum_r, dec_send, dec_recv,
    ):
        pass
    here = hidden[...]
    gained = here * moe_gain[...].astype(F32).reshape(1, SLICE)
    square = jnp.sum(here * here, axis=1, keepdims=True)
    logits = lax.dot_general(
        gained, router_wide[...], (((1,), (1,)), ((), ())),
        precision=lax.Precision.HIGHEST, preferred_element_type=F32,
    )
    lane = lax.broadcasted_iota(jnp.int32, (ROWS, ROWS), 1)
    tables[mp] = jnp.transpose(jnp.where(lane == EXPERTS, square, logits))[0:STATS]
    tables_done = exchange(tables, table_send, table_recv)
    spread((4, 5, 6, 7), (4, 5, 6, 7))
    tables_done()
    total = tables[0]
    for m in range(1, N_MP):
        total = total + tables[m]
    table = jnp.transpose(jnp.concatenate([total, jnp.zeros((ROWS - STATS, ROWS), F32)], axis=0))
    rms = lax.rsqrt(table[:, EXPERTS:EXPERTS + 1] / WIDTH + EPSILON)
    normed = (gained * rms).astype(BF16)
    head = jnp.dot(picks[0], normed, preferred_element_type=F32)
    packed[:, :, 0:SLICE] = head.astype(BF16).reshape(EXPERTS, MSG_ROWS, SLICE)
    tail = jnp.dot(picks[1], normed, preferred_element_type=F32)
    upper = (lax.broadcasted_iota(jnp.int32, (EXPERTS * MSG_ROWS, ROWS), 0) // 8) % 2
    tail = jnp.where(upper[:, 0:1] == 0, tail[:, 0:HALF], tail[:, HALF:SLICE])
    packed[:, :, SLICE:MSG_LANES] = tail.astype(BF16).reshape(EXPERTS, MSG_ROWS, HALF)


    own = pltpu.make_async_copy(packed.at[dp], full.at[mp, SELF // PER, SELF % PER], disp_recv.at[SELF // PER])
    own.start()

    def dispatch(order, carry):
        dest = dest_of(order)
        chunk, place = order // PER, order % PER
        remote(packed.at[dest], full.at[mp, chunk, place], disp_send, disp_recv.at[chunk], (dest, mp)).start()
        return carry

    lax.fori_loop(0, SELF, dispatch, 0)
    lax.fori_loop(SELF + 1, AHEAD * PER, dispatch, 0)

    expert_col = lax.broadcasted_iota(jnp.int32, (ROWS, EXPERTS), 1)
    named_col = [jnp.where(expert_col == id_cols[k], 1.0, 0.0) for k in range(2)]
    logits = [rms * jnp.sum(named_col[k] * table[:, 0:EXPERTS], axis=1, keepdims=True) for k in range(2)]
    top = jnp.maximum(logits[0], logits[1])
    raised = [jnp.exp(value - top) for value in logits]
    place = lax.broadcasted_iota(jnp.int32, (ROWS, EXPERTS * MSG_ROWS), 1)
    gate_head = jnp.zeros(place.shape, F32)
    gate_low = jnp.zeros(place.shape, F32)
    gate_high = jnp.zeros(place.shape, F32)
    for k in range(2):
        gate = raised[k] / (raised[0] + raised[1])
        slot = slot_cols[k]
        base = id_cols[k] * MSG_ROWS
        head_at = jnp.where(slot < MSG_ROWS, base + slot, -1)
        tail_at = jnp.where(slot >= MSG_ROWS, base + slot - MSG_ROWS, -100)
        gate_head = gate_head + jnp.where(place == head_at, gate, 0.0)
        gate_low = gate_low + jnp.where(place == tail_at, gate, 0.0)
        gate_high = gate_high + jnp.where(place == tail_at + 8, gate, 0.0)

    for i, weights in enumerate((gate_head, gate_low, gate_high)):
        main = weights.astype(BF16)
        gated[2 * i] = main
        gated[2 * i + 1] = (weights - main.astype(F32)).astype(BF16)

    def shared_copy(ref, send, recv, kind, k):
        place, device = ((mp, sibling), (mp, pair_a), (m_a, sibling))[kind]
        return remote(ref.at[place, k], ref.at[place, k], send.at[kind, k], recv.at[kind, k], device)

    slot_copy = functools.partial(shared_copy, full, slot_send, slot_recv)
    inner_copy = functools.partial(shared_copy, inner, inner_send, inner_recv)

    def cross_copy(kind, k):
        src, dst = ((part_out, part_in), (last_out, last_in))[kind]
        return remote(src.at[k], dst.at[k], cross_send.at[kind, k], cross_recv.at[kind, k], pair_b)

    def arrive(k):
        @pl.when(k + AHEAD < CHUNKS)
        def _():
            first = (k + AHEAD) * PER
            lax.fori_loop(first, first + PER, dispatch, 0)

        pltpu.make_async_copy(full.at[mp, k], full.at[mp, k], disp_recv.at[k]).wait()
        for kind in (1, 0):
            slot_copy(kind, k).start()

    def forward(copy, k):
        copy(1, k).wait_recv()
        copy(2, k).start()

    rows = PER * MSG_ROWS

    def first_product(k):
        @pl.when(k == 0)
        def _():
            for piece in range(8):
                in_copy(piece).wait_recv()

        slot_copy(0, k).wait_recv()
        slot_copy(2, k).wait_recv()
        order = (x * 2, x * 2 + 1, x_a * 2, x_a * 2 + 1)

        def product(side):
            low = jnp.zeros((2 * rows, FF_SLICE), F32)
            high = jnp.zeros((2 * rows, FF_SLICE), F32)
            for j, m in enumerate(order):
                block = full[m, k].reshape(rows, MSG_LANES)
                end = block[:, SLICE:]
                low = low + jnp.dot(
                    jnp.concatenate([block[:, 0:HALF], end], axis=0),
                    w_in[side, j * SLICE:j * SLICE + HALF],
                    preferred_element_type=F32,
                )
                high = high + jnp.dot(
                    jnp.concatenate([block[:, HALF:SLICE], end], axis=0),
                    w_in[side, j * SLICE + HALF:(j + 1) * SLICE],
                    preferred_element_type=F32,
                )
            ends = (
                low[rows:].reshape(PER, MSG_ROWS, FF_SLICE)[:, 0:8]
                + high[rows:].reshape(PER, MSG_ROWS, FF_SLICE)[:, 8:16]
            )
            return jnp.concatenate([low[:rows] + high[:rows], ends.reshape(PER * 8, FF_SLICE)], axis=0)

        part_out[k] = product(1).astype(BF16)
        cross_copy(0, k).start()
        part_own[k] = product(0)

    def activate(k):
        cross_copy(0, k).wait_recv()
        before = part_own[k] + part_in[k].astype(F32)
        inner[mp, k] = jax.nn.gelu(before, approximate=True).astype(BF16)
        for kind in (1, 0):
            inner_copy(kind, k).start()

    def second_product(k):
        @pl.when(k == 0)
        def _():
            for kind in range(3):
                for piece in range(4):
                    out_copy(kind, piece).wait_recv()

        inner_copy(0, k).wait_recv()
        inner_copy(2, k).wait_recv()

        def product(ref, which):
            out = jnp.zeros((PER * CAP, SLICE), F32)
            for j, m in enumerate((mp, m_sib, m_a, m_a_sib)):
                out = out + jnp.dot(inner[m, k], w_out[j, which], preferred_element_type=F32)
            ref[k, :, :, 0:SLICE] = out[:rows].astype(ref.dtype).reshape(PER, MSG_ROWS, SLICE)
            ends = out[rows:].reshape(PER, 8, SLICE)
            ends = jnp.concatenate([ends[:, :, 0:HALF], ends[:, :, HALF:SLICE]], axis=1)
            ref[k, :, :, SLICE:MSG_LANES] = ends.astype(ref.dtype)

        product(last_out, 1)
        cross_copy(1, k).start()
        product(last_own, 0)

    def finish(k):
        cross_copy(1, k).wait_recv()
        done[k] = (last_own[k] + last_in[k].astype(F32)).astype(BF16)
        for j in range(PER):
            order = k * PER + j
            origin = origin_of(order)
            if j == SELF % PER:
                @pl.when(order == SELF)
                def _():
                    pltpu.make_async_copy(done.at[k, j], back.at[dp], ret_recv).start()

                @pl.when(order != SELF)
                def _():
                    remote(done.at[k, j], back.at[dp], ret_send, ret_recv, (origin, mp)).start()
            else:
                remote(done.at[k, j], back.at[dp], ret_send, ret_recv, (origin, mp)).start()
        for kind in range(3):
            slot_copy(kind, k).wait_send()
            inner_copy(kind, k).wait_send()
        for kind in range(2):
            cross_copy(kind, k).wait_send()

    stages = (
        arrive, functools.partial(forward, slot_copy), first_product, activate,
        functools.partial(forward, inner_copy), second_product, finish,
    )

    def step(i, carry):
        for lag, stage in zip(LAGS, stages):
            @pl.when((i >= lag) & (i - lag < CHUNKS))
            def _():
                stage(i - lag)
        return carry

    lax.fori_loop(0, CHUNKS + LAGS[-1], step, 0)

    for drain in drains:
        drain()
    for kind in range(11):
        gather_copy(kind).wait_send()
    for piece in range(8):
        in_copy(piece).wait_send()
    for kind in range(3):
        for piece in range(4):
            out_copy(kind, piece).wait_send()

    pltpu.make_async_copy(back, back, ret_recv).wait()

    def weigh(i, values):
        return jnp.dot(gated[2 * i], values, preferred_element_type=F32) + jnp.dot(
            gated[2 * i + 1], values, preferred_element_type=F32
        )

    results = back[...].reshape(EXPERTS * MSG_ROWS, MSG_LANES)
    ends = results[:, SLICE:]
    moe = weigh(0, results[:, 0:SLICE])
    mixed[:, 0:HALF] = (hidden[:, 0:HALF] + moe[:, 0:HALF] + weigh(1, ends)).astype(BF16)
    mixed[:, HALF:] = (hidden[:, HALF:] + moe[:, HALF:] + weigh(2, ends)).astype(BF16)

    most = packed.at[pl.ds(0, N_DP - 1)]
    remote(most, most, disp_send, disp_recv.at[0], sibling).wait_send()
    remote(most, most, ret_send, ret_recv, sibling).wait_send()


def call(*operands):
    vmem = pl.BlockSpec(memory_space=pltpu.VMEM)
    hbm = pl.BlockSpec(memory_space=pltpu.HBM)
    dma = pltpu.SemaphoreType.DMA
    block = (PER, MSG_ROWS, MSG_LANES)
    sums = [
        pltpu.VMEM((PARTS, NX, PART, SLICE), BF16),
        pltpu.VMEM((PARTS, NX, PART, SLICE), BF16),
        pltpu.VMEM((PARTS, NX, PART, SLICE), BF16),
        pltpu.VMEM((PARTS, PART, SLICE), BF16),
        pltpu.VMEM((PARTS, PART, SLICE), BF16),
        pltpu.VMEM((PARTS, PART, SLICE), BF16),
    ]
    landing = [
        pltpu.SMEM(o.shape, o.dtype) if o.shape == (1,) else pltpu.VMEM(o.shape, o.dtype) for o in operands[:-2]
    ] + [pltpu.VMEM((2, WIDTH // 2, FF_SLICE), BF16), pltpu.VMEM((4, 2, FF_SLICE, SLICE), BF16)]
    return pl.pallas_call(
        kernel,
        out_shape=jax.ShapeDtypeStruct((2, ROWS, SLICE), BF16),
        in_specs=[hbm] * len(operands),
        out_specs=vmem,
        scratch_shapes=landing + [
            pltpu.VMEM((ROWS, SLICE), F32),
            pltpu.VMEM((N_MP, PARTS, PART, SLICE), BF16),
            pltpu.VMEM((N_MP, 8, ROWS), F32),
            pltpu.VMEM((N_MP, STATS, ROWS), F32),
            pltpu.VMEM((ROWS, SLICE), F32),
            pltpu.VMEM((ROWS, SLICE), F32),
            pltpu.VMEM((2, EXPERTS * MSG_ROWS, ROWS), BF16),
            pltpu.VMEM((6, ROWS, EXPERTS * MSG_ROWS), BF16),
        ] + sums + sums + [
            pltpu.VMEM((EXPERTS, MSG_ROWS, MSG_LANES), BF16),
            pltpu.VMEM((N_MP, CHUNKS) + block, BF16),
            pltpu.VMEM((CHUNKS, PER * CAP, FF_SLICE), BF16),
            pltpu.VMEM((CHUNKS, PER * CAP, FF_SLICE), BF16),
            pltpu.VMEM((CHUNKS, PER * CAP, FF_SLICE), F32),
            pltpu.VMEM((N_MP, CHUNKS, PER * CAP, FF_SLICE), BF16),
            pltpu.VMEM((CHUNKS,) + block, BF16),
            pltpu.VMEM((CHUNKS,) + block, BF16),
            pltpu.VMEM((CHUNKS,) + block, F32),
            pltpu.VMEM((CHUNKS,) + block, BF16),
            pltpu.VMEM((EXPERTS, MSG_ROWS, MSG_LANES), BF16),
            dma((len(operands) + 2,)),
            dma((5, PARTS)),
            dma((5, PARTS)),
            dma((5, PARTS)),
            dma((5, PARTS)),
            dma((11,)),
            dma((11,)),
            dma((N_MP,)),
            dma((N_MP,)),
            dma((N_MP,)),
            dma((N_MP,)),
            dma,
            dma((CHUNKS,)),
            dma((3, CHUNKS)),
            dma((3, CHUNKS)),
            dma((3, CHUNKS)),
            dma((3, CHUNKS)),
            dma((2, CHUNKS)),
            dma((2, CHUNKS)),
            dma((8,)),
            dma((8,)),
            dma((3, 4)),
            dma((3, 4)),
            dma,
            dma,
        ],
        compiler_params=pltpu.CompilerParams(
            collective_id=1, has_side_effects=True, vmem_limit_bytes=VMEM_LIMIT
        ),
        name="whole",
    )(*operands)


def local(
    enc_context, enc_resid, enc_out_w, final_gain, kv_weight, img_queries, img_resid, dec_out_w,
    moe_gain, router_w, expert_ids, text_lengths, expert_in, expert_out,
):
    both = call(
        enc_context, enc_out_w, enc_resid, final_gain, kv_weight, router_w.T, expert_ids.T, img_queries, img_resid,
        moe_gain, text_lengths, dec_out_w, expert_in[0], expert_out[0],
    )
    return both[0], both[1]


def solution(mesh):
    placed = (
        P("dp", "mp"),
        P("dp", "mp"),
        P("mp", None),
        P("mp"),
        P(None, None, "mp"),
        P("dp", "mp"),
        P("dp", "mp"),
        P("mp", None),
        P("mp"),
        P("mp", None),
        P("dp", None),
        P("dp"),
        P("dp", None, "mp"),
        P("dp", "mp", None),
    )
    return jax.shard_map(
        local, mesh=mesh, in_specs=placed, out_specs=(P("dp", "mp"), P("dp", "mp")), check_vma=False
    )
```

```python
import functools
import jax
import jax.numpy as jnp
from jax import lax
from jax.experimental import pallas as pl
from jax.experimental.pallas import tpu as pltpu
from jax.sharding import PartitionSpec as P

HD = 64
EPSILON = 1e-06
SCORE_SCALE = 0.125
MESH = pl.DeviceIdType.MESH
NZ, NY, NX = 8, 4, 4
N_DP, N_MP = NZ * NY, NX * 2
EXPERTS = 32
WIDTH = 4096
SLICE = WIDTH // N_MP
ROWS = 128
FF_SLICE = 256
MSG_ROWS, MSG_LANES, CAP = 16, 768, 24
HALF = SLICE // 2
CHUNKS = 16
PER = N_DP // CHUNKS
F32, BF16 = jnp.float32, jnp.bfloat16
VMEM_LIMIT = 56 * 2**20


def remote(src, dst, send, recv, device):
    return pltpu.make_async_remote_copy(
        src_ref=src, dst_ref=dst, send_sem=send, recv_sem=recv, device_id=device, device_id_type=MESH
    )


def offset_of(order):
    high, place = order // 16, order % 8
    place = (1 - high) * place + high * (7 - place)
    kind, place = place // 4, place % 4
    odd = place % 2
    reach = 1 + kind + 2 * (place // 2)
    dz = ((1 - odd) * reach + odd * (NZ - reach)) * (1 - kind * (place // 3))
    return dz, order // 8


SPREAD = FF_SLICE // 2
PARTS = 2
PART = ROWS // PARTS
STATS = 40
AHEAD = 6
SELF = 7
LAGS = (0, 3, 4, 6, 9, 10, 13)


def kernel(*refs):
    sources, rest = refs[:14], refs[14:]
    (
        both,
        enc_context, enc_w, enc_resid, final_gain, kv_w, router, ids_row, img_queries, img_resid, moe_gain,
        lengths, dec_w, w_in, w_out,
        state, gathered, squares, tables, hidden, router_wide, picks, gated,
        enc_give, enc_kept, enc_taken, enc_sum_f, enc_sum_l, enc_sum_r,
        dec_give, dec_kept, dec_taken, dec_sum_f, dec_sum_l, dec_sum_r,
        packed, full, part_out, part_in, part_own, inner, last_out, last_in, last_own, done, back,
        load_sem, enc_send, enc_recv, dec_send, dec_recv, ag_send, ag_recv,
        square_send, square_recv, table_send, table_recv,
        disp_send, disp_recv, slot_send, slot_recv, inner_send, inner_recv, cross_send, cross_recv,
        in_send, in_recv, out_send, out_recv, ret_send, ret_recv,
    ) = rest
    targets = rest[1:15]
    encoded, mixed = both.at[0], both.at[1]
    dp, mp = lax.axis_index("dp"), lax.axis_index("mp")
    z, y = dp // NY, dp % NY
    x, core = mp // 2, mp % 2
    x_right, x_left, x_far = (x + 1) % NX, (x + NX - 1) % NX, (x + 2) % NX
    m_right, m_left, m_far = x_right * 2 + core, x_left * 2 + core, x_far * 2 + core
    sibling, right, left, far = (dp, x * 2 + 1 - core), (dp, m_right), (dp, m_left), (dp, m_far)

    def dest_of(order):
        dz, dy = offset_of(order)
        return ((z + dz) % NZ) * NY + (y + dy) % NY

    def origin_of(order):
        dz, dy = offset_of(order)
        return ((z + NZ - dz) % NZ) * NY + (y + NY - dy) % NY

    loads = [
        pltpu.make_async_copy(src, dst, load_sem.at[i])
        for i, (src, dst) in enumerate(zip(sources[:-2], targets))
    ]
    w_in_hbm, w_out_hbm = sources[-2:]

    x_a, x_b = NX - 1 - x, x + 1 - 2 * (x % 2)
    m_a, m_b, m_sib = x_a * 2 + core, x_b * 2 + core, x * 2 + 1 - core
    m_a_sib = x_a * 2 + 1 - core
    pair_a, pair_b = (dp, m_a), (dp, m_b)
    chip = 2 * SLICE

    def in_rows(of, start, count):
        return w_in_hbm.at[pl.ds(pl.multiple_of(of * chip + start, 128), count)]

    def out_block(part, m):
        return w_out_hbm.at[pl.ds(part * SPREAD, SPREAD), pl.ds(pl.multiple_of(m * SLICE, SLICE), SLICE)]

    def out_whole(m):
        return w_out_hbm.at[:, pl.ds(pl.multiple_of(m * SLICE, SLICE), SLICE)]

    count = len(sources)
    loads += [
        pltpu.make_async_copy(in_rows(x, 0, chip), w_in.at[0, pl.ds(0, chip)], load_sem.at[count - 2]),
        pltpu.make_async_copy(in_rows(x_a, 0, chip), w_in.at[0, pl.ds(chip, chip)], load_sem.at[count - 1]),
        pltpu.make_async_copy(out_whole(mp), w_out.at[0, 0], load_sem.at[count]),
        pltpu.make_async_copy(out_whole(m_b), w_out.at[0, 1], load_sem.at[count + 1]),
    ]

    def in_copy(piece):
        side, start = piece // 4, piece % 4 * FF_SLICE
        of = x_b if side == 0 else NX - 1 - x_b
        return remote(
            in_rows(of, start, FF_SLICE), w_in.at[1, pl.ds(side * chip + start, FF_SLICE)],
            in_send.at[piece], in_recv.at[piece], pair_b,
        )

    def out_copy(kind, piece):
        to = (m_sib, m_a, m_a_sib)[kind]
        which, part = piece // 2, piece % 2
        to_chip = to // 2
        m = to if which == 0 else (to_chip + 1 - 2 * (to_chip % 2)) * 2 + to % 2
        return remote(
            out_block(part, m), w_out.at[kind + 1, which, pl.ds(part * SPREAD, SPREAD)],
            out_send.at[kind, piece], out_recv.at[kind, piece], (dp, to),
        )

    def spread(ins, outs):
        for piece, unit in zip(ins, outs):
            in_copy(piece).start()
            out_copy(1 + unit % 2, unit // 2).start()

    for load in loads[:3]:
        load.start()
    barrier = pltpu.get_barrier_semaphore()
    for o in range(1, N_MP):
        pl.semaphore_signal(barrier, inc=1, device_id=(dp, (mp + o) % N_MP), device_id_type=MESH)

    def greet(order, carry):
        pl.semaphore_signal(barrier, inc=1, device_id=(dest_of(order), mp), device_id_type=MESH)
        return carry

    lax.fori_loop(0, SELF, greet, 0)
    lax.fori_loop(SELF + 1, N_DP, greet, 0)
    for load in loads[3:]:
        load.start()

    def reduce_scatter(values, weights, resid, out, give, kept, taken, sum_f, sum_l, sum_r, send, recv):
        def copy(kind, r):
            src, dst, device = {
                0: (give.at[r], taken.at[r], sibling),
                1: (kept.at[r, x_far], sum_f.at[r], far),
                2: (kept.at[r, x_right], sum_l.at[r], right),
                3: (kept.at[r, x_left], sum_r.at[r], left),
            }[kind]
            return remote(src, dst, send.at[kind, r], recv.at[kind, r], device)

        def product(ref, r, px, side):
            at = pl.multiple_of((px * 2 + side) * SLICE, SLICE)
            ref[r, px] = jnp.dot(
                values[r * PART:(r + 1) * PART], weights[:, pl.ds(at, SLICE)], preferred_element_type=F32
            ).astype(BF16)

        def pair(r, px, rows=slice(None)):
            return kept[r, px, rows].astype(F32) + taken[r, px, rows].astype(F32)

        for r in range(PARTS):
            for px in range(NX):
                product(give, r, px, 1 - core)
            if r == 0 and out is state:
                pl.semaphore_wait(barrier, N_MP - 1 + N_DP - 1)
            copy(0, r).start()
            if r == 0 and out is state:
                spread((0,), (0,))
                for piece in range(4):
                    out_copy(0, piece).start()
        for r in range(PARTS):
            for px in range(NX):
                product(kept, r, px, core)
        for r in range(PARTS):
            copy(0, r).wait_recv()
            for kind, px in ((1, x_far), (2, x_right), (3, x_left)):
                kept[r, px] = pair(r, px).astype(BF16)
                copy(kind, r).start()
        for r in range(PARTS):
            rows = slice(r * PART, (r + 1) * PART)
            base = resid[rows].astype(F32) + pair(r, x)
            for kind in (2, 3, 1):
                copy(kind, r).wait_recv()
            out[rows] = base + sum_l[r].astype(F32) + sum_r[r].astype(F32) + sum_f[r].astype(F32)
            yield r

        def drain():
            for r in range(PARTS):
                for kind in range(4):
                    copy(kind, r).wait_send()

        drains.append(drain)

    drains = []

    def exchange(ref, send, recv):
        def copy(o):
            return remote(ref.at[mp], ref.at[mp], send.at[o], recv.at[mp], (dp, (mp + o) % N_MP))

        for o in range(1, N_MP):
            copy(o).start()

        def finish():
            for o in range(1, N_MP):
                other = ref.at[(mp + o) % N_MP]
                remote(other, other, send.at[o], recv.at[(mp + o) % N_MP], sibling).wait_recv()
            drains.append(lambda: [copy(o).wait_send() for o in range(1, N_MP)])

        return finish

    def gather_copy(kind):
        ref, device = {
            0: (gathered.at[mp, 0], sibling), 1: (gathered.at[mp, 1], sibling),
            2: (gathered.at[mp, 0], right), 3: (gathered.at[mp, 1], right),
            4: (gathered.at[mp, 0], left), 5: (gathered.at[mp, 1], left),
            6: (gathered.at[mp, 0], far), 7: (gathered.at[mp, 1], far),
            8: (gathered.at[m_left], sibling), 9: (gathered.at[m_right], sibling),
            10: (gathered.at[m_far], sibling),
        }[kind]
        return remote(ref, ref, ag_send.at[kind], ag_recv.at[kind], device)

    for load in loads[:4]:
        load.wait()
    text_gain = final_gain[...].astype(F32).reshape(1, SLICE)
    for r in reduce_scatter(
        enc_context[...], enc_w, enc_resid, state, enc_give, enc_kept, enc_taken, enc_sum_f,
        enc_sum_l, enc_sum_r, enc_send, enc_recv,
    ):
        gathered[mp, r] = (state[r * PART:(r + 1) * PART] * text_gain).astype(BF16)
        for kind in ((6, 2, 4, 0), (7, 3, 5, 1))[r]:
            gather_copy(kind).start()
    text_state = state[...]
    square = jnp.sum(text_state * text_state, axis=1, keepdims=True)
    squares[mp] = jnp.transpose(jnp.broadcast_to(square, (ROWS, ROWS)))[0:8]
    squares_done = exchange(squares, square_send, square_recv)

    for load in loads[4:]:
        load.wait()
    row_at = lax.broadcasted_iota(jnp.int32, (ROWS, ROWS), 0)
    col_at = lax.broadcasted_iota(jnp.int32, (ROWS, ROWS), 1)
    expert_row = lax.broadcasted_iota(jnp.int32, (EXPERTS, ROWS), 0)
    named_row = [jnp.where(expert_row == ids_row[k:k + 1, :], 1.0, 0.0) for k in range(2)]
    earlier_row = jnp.dot(
        (named_row[0] + named_row[1]).astype(BF16),
        jnp.where(row_at < col_at, 1.0, 0.0).astype(BF16),
        preferred_element_type=F32,
    )
    message = lax.broadcasted_iota(jnp.int32, (EXPERTS * MSG_ROWS, ROWS), 0)
    upper = (message // 8) % 2
    pick_head = jnp.zeros((EXPERTS * MSG_ROWS, ROWS), F32)
    pick_tail = jnp.zeros((EXPERTS * MSG_ROWS, ROWS), F32)
    slots = []
    for k in range(2):
        slot = jnp.sum(named_row[k] * earlier_row, axis=0, keepdims=True).astype(jnp.int32)
        slots.append(slot.astype(F32))
        base = ids_row[k:k + 1, :] * MSG_ROWS
        head_at = jnp.where(slot < MSG_ROWS, base + slot, -1)
        tail_at = jnp.where(slot >= MSG_ROWS, base + slot - MSG_ROWS, -1)
        pick_head = pick_head + jnp.where(message == head_at, 1.0, 0.0)
        pick_tail = pick_tail + jnp.where(message - 8 * upper == tail_at, 1.0, 0.0)
    picks[0] = pick_head.astype(BF16)
    picks[1] = pick_tail.astype(BF16)
    columns = jnp.transpose(
        jnp.concatenate([ids_row[...].astype(F32)] + slots + [jnp.zeros((ROWS - 4, ROWS), F32)], axis=0)
    )
    id_cols = [columns[:, k:k + 1].astype(jnp.int32) for k in range(2)]
    slot_cols = [columns[:, 2 + k:3 + k].astype(jnp.int32) for k in range(2)]
    router_wide[...] = jnp.zeros(router_wide.shape, F32)
    router_wide[0:EXPERTS] = router[...].astype(F32)

    sums = [jnp.zeros((ROWS, FF_SLICE), F32) for _ in range(2)]

    def project(m):
        at = pl.multiple_of(m * SLICE, SLICE)
        block = gathered[m].reshape(ROWS, SLICE)
        for which in range(2):
            sums[which] = sums[which] + jnp.dot(
                block, kv_w[which, pl.ds(at, SLICE), :], preferred_element_type=F32
            )

    project(mp)
    for kinds, on in (((2, 3), 8), ((4, 5), 9), ((6, 7), 10)):
        for kind in kinds:
            gather_copy(kind).wait_recv()
        gather_copy(on).start()
    spread((1, 2, 3), (1, 2, 3))
    project(m_left)
    project(m_right)
    gather_copy(0).wait_recv()
    gather_copy(1).wait_recv()
    project(x * 2 + 1 - core)
    project(m_far)
    for kind, px in ((8, x_left), (9, x_right), (10, x_far)):
        gather_copy(kind).wait_recv()
        project(px * 2 + 1 - core)
    squares_done()
    total = squares[0]
    for m in range(1, N_MP):
        total = total + squares[m]
    total = jnp.transpose(jnp.concatenate([total, jnp.zeros((ROWS - 8, ROWS), F32)], axis=0))[:, 0:1]
    text_scale = lax.rsqrt(total / WIDTH + EPSILON)
    encoded[...] = (state[...] * text_gain * text_scale).astype(BF16)
    keys = (sums[0] * text_scale).astype(BF16)
    values = (sums[1] * text_scale).astype(BF16)

    heads = FF_SLICE // HD
    head_of = lax.broadcasted_iota(jnp.int32, (ROWS, FF_SLICE), 1) // HD
    queries = img_queries[...]
    alone = jnp.concatenate([jnp.where(head_of == h, queries, jnp.zeros_like(queries)) for h in range(heads)], axis=0)
    scores = SCORE_SCALE * lax.dot_general(
        alone, keys, (((1,), (1,)), ((), ())), preferred_element_type=F32
    )
    valid = lax.broadcasted_iota(jnp.int32, scores.shape, 1) < lengths[0]
    scores = jnp.where(valid, scores, -jnp.inf)
    raised = jnp.exp(scores - jnp.max(scores, axis=1, keepdims=True))
    probs = (raised / jnp.sum(raised, axis=1, keepdims=True)).astype(BF16)
    mixed_heads = jnp.dot(probs, values, preferred_element_type=F32)
    context = jnp.zeros((ROWS, FF_SLICE), F32)
    for h in range(heads):
        context = context + jnp.where(head_of == h, mixed_heads[h * ROWS:(h + 1) * ROWS], 0.0)
    context = context.astype(BF16)

    for _ in reduce_scatter(
        context, dec_w, img_resid, hidden, dec_give, dec_kept, dec_taken, dec_sum_f,
        dec_sum_l, dec_sum_r, dec_send, dec_recv,
    ):
        pass
    here = hidden[...]
    gained = here * moe_gain[...].astype(F32).reshape(1, SLICE)
    square = jnp.sum(here * here, axis=1, keepdims=True)
    logits = lax.dot_general(
        gained, router_wide[...], (((1,), (1,)), ((), ())),
        precision=lax.Precision.HIGHEST, preferred_element_type=F32,
    )
    lane = lax.broadcasted_iota(jnp.int32, (ROWS, ROWS), 1)
    tables[mp] = jnp.transpose(jnp.where(lane == EXPERTS, square, logits))[0:STATS]
    tables_done = exchange(tables, table_send, table_recv)
    spread((4, 5, 6, 7), (4, 5, 6, 7))
    tables_done()
    total = tables[0]
    for m in range(1, N_MP):
        total = total + tables[m]
    table = jnp.transpose(jnp.concatenate([total, jnp.zeros((ROWS - STATS, ROWS), F32)], axis=0))
    rms = lax.rsqrt(table[:, EXPERTS:EXPERTS + 1] / WIDTH + EPSILON)
    normed = (gained * rms).astype(BF16)
    head = jnp.dot(picks[0], normed, preferred_element_type=F32)
    packed[:, :, 0:SLICE] = head.astype(BF16).reshape(EXPERTS, MSG_ROWS, SLICE)
    tail = jnp.dot(picks[1], normed, preferred_element_type=F32)
    upper = (lax.broadcasted_iota(jnp.int32, (EXPERTS * MSG_ROWS, ROWS), 0) // 8) % 2
    tail = jnp.where(upper[:, 0:1] == 0, tail[:, 0:HALF], tail[:, HALF:SLICE])
    packed[:, :, SLICE:MSG_LANES] = tail.astype(BF16).reshape(EXPERTS, MSG_ROWS, HALF)


    own = pltpu.make_async_copy(packed.at[dp], full.at[mp, SELF // PER, SELF % PER], disp_recv.at[SELF // PER])
    own.start()

    def dispatch(order, carry):
        dest = dest_of(order)
        chunk, place = order // PER, order % PER
        remote(packed.at[dest], full.at[mp, chunk, place], disp_send, disp_recv.at[chunk], (dest, mp)).start()
        return carry

    lax.fori_loop(0, SELF, dispatch, 0)
    lax.fori_loop(SELF + 1, AHEAD * PER, dispatch, 0)

    expert_col = lax.broadcasted_iota(jnp.int32, (ROWS, EXPERTS), 1)
    named_col = [jnp.where(expert_col == id_cols[k], 1.0, 0.0) for k in range(2)]
    logits = [rms * jnp.sum(named_col[k] * table[:, 0:EXPERTS], axis=1, keepdims=True) for k in range(2)]
    top = jnp.maximum(logits[0], logits[1])
    raised = [jnp.exp(value - top) for value in logits]
    place = lax.broadcasted_iota(jnp.int32, (ROWS, EXPERTS * MSG_ROWS), 1)
    gate_head = jnp.zeros(place.shape, F32)
    gate_low = jnp.zeros(place.shape, F32)
    gate_high = jnp.zeros(place.shape, F32)
    for k in range(2):
        gate = raised[k] / (raised[0] + raised[1])
        slot = slot_cols[k]
        base = id_cols[k] * MSG_ROWS
        head_at = jnp.where(slot < MSG_ROWS, base + slot, -1)
        tail_at = jnp.where(slot >= MSG_ROWS, base + slot - MSG_ROWS, -100)
        gate_head = gate_head + jnp.where(place == head_at, gate, 0.0)
        gate_low = gate_low + jnp.where(place == tail_at, gate, 0.0)
        gate_high = gate_high + jnp.where(place == tail_at + 8, gate, 0.0)

    for i, weights in enumerate((gate_head, gate_low, gate_high)):
        main = weights.astype(BF16)
        gated[2 * i] = main
        gated[2 * i + 1] = (weights - main.astype(F32)).astype(BF16)

    def shared_copy(ref, send, recv, kind, k):
        place, device = ((mp, sibling), (mp, pair_a), (m_a, sibling))[kind]
        return remote(ref.at[place, k], ref.at[place, k], send.at[kind, k], recv.at[kind, k], device)

    slot_copy = functools.partial(shared_copy, full, slot_send, slot_recv)
    inner_copy = functools.partial(shared_copy, inner, inner_send, inner_recv)

    def cross_copy(kind, k):
        src, dst = ((part_out, part_in), (last_out, last_in))[kind]
        return remote(src.at[k], dst.at[k], cross_send.at[kind, k], cross_recv.at[kind, k], pair_b)

    def arrive(k):
        @pl.when(k + AHEAD < CHUNKS)
        def _():
            first = (k + AHEAD) * PER
            lax.fori_loop(first, first + PER, dispatch, 0)

        pltpu.make_async_copy(full.at[mp, k], full.at[mp, k], disp_recv.at[k]).wait()
        for kind in (1, 0):
            slot_copy(kind, k).start()

    def forward(copy, k):
        copy(1, k).wait_recv()
        copy(2, k).start()

    rows = PER * MSG_ROWS

    def first_product(k):
        @pl.when(k == 0)
        def _():
            for piece in range(8):
                in_copy(piece).wait_recv()

        slot_copy(0, k).wait_recv()
        slot_copy(2, k).wait_recv()
        order = (x * 2, x * 2 + 1, x_a * 2, x_a * 2 + 1)

        def product(side):
            low = jnp.zeros((2 * rows, FF_SLICE), F32)
            high = jnp.zeros((2 * rows, FF_SLICE), F32)
            for j, m in enumerate(order):
                block = full[m, k].reshape(rows, MSG_LANES)
                end = block[:, SLICE:]
                low = low + jnp.dot(
                    jnp.concatenate([block[:, 0:HALF], end], axis=0),
                    w_in[side, j * SLICE:j * SLICE + HALF],
                    preferred_element_type=F32,
                )
                high = high + jnp.dot(
                    jnp.concatenate([block[:, HALF:SLICE], end], axis=0),
                    w_in[side, j * SLICE + HALF:(j + 1) * SLICE],
                    preferred_element_type=F32,
                )
            ends = (
                low[rows:].reshape(PER, MSG_ROWS, FF_SLICE)[:, 0:8]
                + high[rows:].reshape(PER, MSG_ROWS, FF_SLICE)[:, 8:16]
            )
            return jnp.concatenate([low[:rows] + high[:rows], ends.reshape(PER * 8, FF_SLICE)], axis=0)

        part_out[k] = product(1).astype(BF16)
        cross_copy(0, k).start()
        part_own[k] = product(0)

    def activate(k):
        cross_copy(0, k).wait_recv()
        before = part_own[k] + part_in[k].astype(F32)
        inner[mp, k] = jax.nn.gelu(before, approximate=True).astype(BF16)
        for kind in (1, 0):
            inner_copy(kind, k).start()

    def second_product(k):
        @pl.when(k == 0)
        def _():
            for kind in range(3):
                for piece in range(4):
                    out_copy(kind, piece).wait_recv()

        inner_copy(0, k).wait_recv()
        inner_copy(2, k).wait_recv()

        def product(ref, which):
            out = jnp.zeros((PER * CAP, SLICE), F32)
            for j, m in enumerate((mp, m_sib, m_a, m_a_sib)):
                out = out + jnp.dot(inner[m, k], w_out[j, which], preferred_element_type=F32)
            ref[k, :, :, 0:SLICE] = out[:rows].astype(ref.dtype).reshape(PER, MSG_ROWS, SLICE)
            ends = out[rows:].reshape(PER, 8, SLICE)
            ends = jnp.concatenate([ends[:, :, 0:HALF], ends[:, :, HALF:SLICE]], axis=1)
            ref[k, :, :, SLICE:MSG_LANES] = ends.astype(ref.dtype)

        product(last_out, 1)
        cross_copy(1, k).start()
        product(last_own, 0)

    def finish(k):
        cross_copy(1, k).wait_recv()
        done[k] = (last_own[k] + last_in[k].astype(F32)).astype(BF16)
        for j in range(PER):
            order = k * PER + j
            origin = origin_of(order)
            if j == SELF % PER:
                @pl.when(order == SELF)
                def _():
                    pltpu.make_async_copy(done.at[k, j], back.at[dp], ret_recv).start()

                @pl.when(order != SELF)
                def _():
                    remote(done.at[k, j], back.at[dp], ret_send, ret_recv, (origin, mp)).start()
            else:
                remote(done.at[k, j], back.at[dp], ret_send, ret_recv, (origin, mp)).start()

    def settle(k, carry):
        for kind in range(3):
            slot_copy(kind, k).wait_send()
            inner_copy(kind, k).wait_send()
        for kind in range(2):
            cross_copy(kind, k).wait_send()
        return carry

    stages = (
        arrive, functools.partial(forward, slot_copy), first_product, activate,
        functools.partial(forward, inner_copy), second_product, finish,
    )

    for drain in drains:
        drain()
    for kind in range(11):
        gather_copy(kind).wait_send()

    def step(i, carry):
        for lag, stage in zip(LAGS, stages):
            @pl.when((i >= lag) & (i - lag < CHUNKS))
            def _():
                stage(i - lag)
        return carry

    lax.fori_loop(0, CHUNKS + LAGS[-1], step, 0)

    lax.fori_loop(0, CHUNKS, settle, 0)
    for piece in range(8):
        in_copy(piece).wait_send()
    for kind in range(3):
        for piece in range(4):
            out_copy(kind, piece).wait_send()

    pltpu.make_async_copy(back, back, ret_recv).wait()

    def weigh(i, values):
        return jnp.dot(gated[2 * i], values, preferred_element_type=F32) + jnp.dot(
            gated[2 * i + 1], values, preferred_element_type=F32
        )

    results = back[...].reshape(EXPERTS * MSG_ROWS, MSG_LANES)
    ends = results[:, SLICE:]
    moe = weigh(0, results[:, 0:SLICE])
    mixed[:, 0:HALF] = (hidden[:, 0:HALF] + moe[:, 0:HALF] + weigh(1, ends)).astype(BF16)
    mixed[:, HALF:] = (hidden[:, HALF:] + moe[:, HALF:] + weigh(2, ends)).astype(BF16)

    most = packed.at[pl.ds(0, N_DP - 1)]
    remote(most, most, disp_send, disp_recv.at[0], sibling).wait_send()
    remote(most, most, ret_send, ret_recv, sibling).wait_send()


def call(*operands):
    vmem = pl.BlockSpec(memory_space=pltpu.VMEM)
    hbm = pl.BlockSpec(memory_space=pltpu.HBM)
    dma = pltpu.SemaphoreType.DMA
    block = (PER, MSG_ROWS, MSG_LANES)
    sums = [
        pltpu.VMEM((PARTS, NX, PART, SLICE), BF16),
        pltpu.VMEM((PARTS, NX, PART, SLICE), BF16),
        pltpu.VMEM((PARTS, NX, PART, SLICE), BF16),
        pltpu.VMEM((PARTS, PART, SLICE), BF16),
        pltpu.VMEM((PARTS, PART, SLICE), BF16),
        pltpu.VMEM((PARTS, PART, SLICE), BF16),
    ]
    landing = [
        pltpu.SMEM(o.shape, o.dtype) if o.shape == (1,) else pltpu.VMEM(o.shape, o.dtype) for o in operands[:-2]
    ] + [pltpu.VMEM((2, WIDTH // 2, FF_SLICE), BF16), pltpu.VMEM((4, 2, FF_SLICE, SLICE), BF16)]
    return pl.pallas_call(
        kernel,
        out_shape=jax.ShapeDtypeStruct((2, ROWS, SLICE), BF16),
        in_specs=[hbm] * len(operands),
        out_specs=vmem,
        scratch_shapes=landing + [
            pltpu.VMEM((ROWS, SLICE), F32),
            pltpu.VMEM((N_MP, PARTS, PART, SLICE), BF16),
            pltpu.VMEM((N_MP, 8, ROWS), F32),
            pltpu.VMEM((N_MP, STATS, ROWS), F32),
            pltpu.VMEM((ROWS, SLICE), F32),
            pltpu.VMEM((ROWS, SLICE), F32),
            pltpu.VMEM((2, EXPERTS * MSG_ROWS, ROWS), BF16),
            pltpu.VMEM((6, ROWS, EXPERTS * MSG_ROWS), BF16),
        ] + sums + sums + [
            pltpu.VMEM((EXPERTS, MSG_ROWS, MSG_LANES), BF16),
            pltpu.VMEM((N_MP, CHUNKS) + block, BF16),
            pltpu.VMEM((CHUNKS, PER * CAP, FF_SLICE), BF16),
            pltpu.VMEM((CHUNKS, PER * CAP, FF_SLICE), BF16),
            pltpu.VMEM((CHUNKS, PER * CAP, FF_SLICE), F32),
            pltpu.VMEM((N_MP, CHUNKS, PER * CAP, FF_SLICE), BF16),
            pltpu.VMEM((CHUNKS,) + block, BF16),
            pltpu.VMEM((CHUNKS,) + block, BF16),
            pltpu.VMEM((CHUNKS,) + block, F32),
            pltpu.VMEM((CHUNKS,) + block, BF16),
            pltpu.VMEM((EXPERTS, MSG_ROWS, MSG_LANES), BF16),
            dma((len(operands) + 2,)),
            dma((5, PARTS)),
            dma((5, PARTS)),
            dma((5, PARTS)),
            dma((5, PARTS)),
            dma((11,)),
            dma((11,)),
            dma((N_MP,)),
            dma((N_MP,)),
            dma((N_MP,)),
            dma((N_MP,)),
            dma,
            dma((CHUNKS,)),
            dma((3, CHUNKS)),
            dma((3, CHUNKS)),
            dma((3, CHUNKS)),
            dma((3, CHUNKS)),
            dma((2, CHUNKS)),
            dma((2, CHUNKS)),
            dma((8,)),
            dma((8,)),
            dma((3, 4)),
            dma((3, 4)),
            dma,
            dma,
        ],
        compiler_params=pltpu.CompilerParams(
            collective_id=1, has_side_effects=True, vmem_limit_bytes=VMEM_LIMIT
        ),
        name="whole",
    )(*operands)


def local(
    enc_context, enc_resid, enc_out_w, final_gain, kv_weight, img_queries, img_resid, dec_out_w,
    moe_gain, router_w, expert_ids, text_lengths, expert_in, expert_out,
):
    both = call(
        enc_context, enc_out_w, enc_resid, final_gain, kv_weight, router_w.T, expert_ids.T, img_queries, img_resid,
        moe_gain, text_lengths, dec_out_w, expert_in[0], expert_out[0],
    )
    return both[0], both[1]


def solution(mesh):
    placed = (
        P("dp", "mp"),
        P("dp", "mp"),
        P("mp", None),
        P("mp"),
        P(None, None, "mp"),
        P("dp", "mp"),
        P("dp", "mp"),
        P("mp", None),
        P("mp"),
        P("mp", None),
        P("dp", None),
        P("dp"),
        P("dp", None, "mp"),
        P("dp", "mp", None),
    )
    return jax.shard_map(
        local, mesh=mesh, in_specs=placed, out_specs=(P("dp", "mp"), P("dp", "mp")), check_vma=False
    )
```
